128 devices in a mesh: tm: 8 (over y, core), ha: 4 (over x), wa: 4 (over z).
Axes of the slice: x: 4, y: 4, z: 4, core: 2. Of those that a mesh axis runs over, the one named last changes fastest.
Arguments:
- frames: bfloat16 [32, 128, 128, 256], P('tm', 'ha', 'wa'), may hold values from -100 to 100
- history: bfloat16 [2, 128, 128, 256], P(None, 'ha', 'wa'), may hold values from -6 to 6
- cotangent: bfloat16 [32, 128, 128, 256], P('tm', 'ha', 'wa'), may hold values from -6 to 6
- space_weight: bfloat16 [3, 3, 256, 256], replicated, may hold values from -0.125 to 0.125
- time_weight: bfloat16 [3, 256, 256], replicated, may hold values from -0.21875 to 0.21875
- norm_gain: float32 [256], replicated, may hold values from 0.1 to 1.9
- norm_shift: float32 [256], replicated, may hold values from -3 to 3
Outputs:
- grad_input: bfloat16 [32, 128, 128, 256], P('tm', 'ha', 'wa')
- space_grad: float32 [3, 3, 256, 256], replicated
- time_grad: float32 [3, 256, 256], replicated
- gain_grad: float32 [256], replicated
- shift_grad: float32 [256], replicated
The draws below stay inside these ranges and needn't reach their ends.
All inputs are finite; a program needn't handle non-finite values.
Results may differ from the reference program's by a relative error of at most 0.007.
Values may be sent and summed in bfloat16 or wider, within the bound.
A program may use at most 128 MiB of HBM per device.

```python
import jax
import jax.numpy as jnp
from jax import lax

C = 256
GROUPS = 32
FRAMES = 32
HEIGHT = 128
WIDTH = 128


def draw_frames(key, part):
    key = jax.random.fold_in(key, 11)
    key_base, key_chan, key_rough = jax.random.split(key, 3)
    shape = (FRAMES, HEIGHT, WIDTH, C)
    frame_pos = jnp.arange(FRAMES, dtype=jnp.float32) / max(FRAMES - 1, 1)
    row_pos = jnp.arange(HEIGHT, dtype=jnp.float32) / max(HEIGHT - 1, 1)
    col_pos = jnp.arange(WIDTH, dtype=jnp.float32) / max(WIDTH - 1, 1)
    ramp = jnp.log(3.0) * (frame_pos[:, None, None] + row_pos[None, :, None] + col_pos[None, None, :] - 1.5)
    rough = jax.random.uniform(key_rough, (FRAMES, HEIGHT, WIDTH), minval=-0.5, maxval=0.5)
    channel_scale = jnp.exp(jax.random.uniform(key_chan, (C,), minval=-0.7, maxval=0.7))
    base = jnp.clip(jax.random.normal(key_base, shape), -4.0, 4.0) + 1.0
    scale = jnp.exp(ramp + rough)
    return (base * scale[..., None] * channel_scale).astype(jnp.bfloat16)


def block_scale(key, shape, pieces, least, top_value):
    loudness, own = 1.0, jax.random.fold_in(key, 6)
    for dim, shards_of in pieces:
        draws = jnp.exp(jax.random.uniform(jax.random.fold_in(own, dim), (shards_of,), jnp.float32, least / len(pieces), top_value / len(pieces)))
        loudness = loudness * jnp.repeat(draws, shape[dim] // shards_of).reshape([-1 if axis == dim else 1 for axis in range(len(shape))])
    return loudness


def bell_draw(rng, extent, width, reach, cuts=(), kind=jnp.bfloat16):
    loudness = block_scale(rng, extent, cuts, -0.22, 0.18) if cuts else 1.0
    array = jax.random.normal(rng, extent, jnp.float32) * width * loudness
    return jnp.minimum(jnp.maximum(array, -reach), reach).astype(kind)


def setup_inputs(seed: int = 0) -> dict:
    key_of = jax.random.split(jax.random.key(seed), 8)
    frames = draw_frames(jax.random.fold_in(key_of[7], 71), 0)
    history = bell_draw(key_of[1], (2, HEIGHT, WIDTH, C), 1.0, 6.0, ((1, 4), (2, 4)))
    cotangent = bell_draw(key_of[2], (FRAMES, HEIGHT, WIDTH, C), 1.0, 6.0, ((0, 8), (1, 4), (2, 4)))
    space_weight = bell_draw(key_of[3], (3, 3, C, C), (9 * C) ** -0.5, 0.125)
    time_weight = bell_draw(key_of[4], (3, C, C), (3 * C) ** -0.5, 0.21875)
    norm_gain = jnp.clip(1.0 + 0.18 * jax.random.normal(key_of[5], (C,), jnp.float32), 0.1, 1.9)
    norm_shift = bell_draw(key_of[6], (C,), 0.5, 3.0, (), jnp.float32)
    return {"frames": frames, "history": history, "cotangent": cotangent, "space_weight": space_weight, "time_weight": time_weight, "norm_gain": norm_gain, "norm_shift": norm_shift}


EPSILON = 1e-05

def silu_grad(value):
    logistic = jax.nn.sigmoid(value)
    return logistic * (1.0 + value * (1.0 - logistic))

def conv_space(padded, weights, row_count, col_count):
    result = jnp.zeros(padded.shape[:1] + (row_count, col_count, weights.shape[3]), jnp.float32)
    for i in range(3):
        for j in range(3):
            result = result + jnp.einsum('fhwc,cd->fhwd', padded[:, i:i + row_count, j:j + col_count].astype(jnp.float32), weights[i, j].astype(jnp.float32))
    return result

def reference(frames, history, cotangent, space_weight, time_weight, norm_gain, norm_shift):
    group_width = C // GROUPS
    padded = jnp.pad(frames, ((0, 0), (1, 1), (1, 1), (0, 0)))
    features = conv_space(padded, space_weight, HEIGHT, WIDTH).astype(jnp.bfloat16)
    extended = jnp.concatenate([history, features], 0)
    temporal = jnp.zeros(frames.shape, jnp.float32)
    for k in range(3):
        temporal = temporal + jnp.einsum('fhwc,cd->fhwd', extended[2 - k:2 - k + FRAMES].astype(jnp.float32), time_weight[k].astype(jnp.float32))
    cell_count = FRAMES * HEIGHT * WIDTH * group_width
    mean_value = lax.optimization_barrier(jnp.sum(temporal, axis=(0, 1, 2))).reshape(GROUPS, group_width).sum(1) / cell_count
    centered = temporal - jnp.repeat(mean_value, group_width)
    variance = lax.optimization_barrier(jnp.sum(centered * centered, axis=(0, 1, 2))).reshape(GROUPS, group_width).sum(1) / cell_count
    inv_std = jnp.repeat(lax.rsqrt(variance + EPSILON), group_width)
    normalized = centered * inv_std
    pre_act = normalized * norm_gain + norm_shift
    grad_pre = cotangent.astype(jnp.float32) * silu_grad(pre_act)
    shift_sum = lax.optimization_barrier(jnp.sum(grad_pre, axis=(0, 1, 2)))
    gain_sum = lax.optimization_barrier(jnp.sum(grad_pre * normalized, axis=(0, 1, 2)))
    grad_norm = grad_pre * norm_gain
    first_sum = (norm_gain * shift_sum).reshape(GROUPS, group_width).sum(1)
    second_sum = (norm_gain * gain_sum).reshape(GROUPS, group_width).sum(1)
    grad_temporal = (inv_std * (grad_norm - jnp.repeat(first_sum, group_width) / cell_count - normalized * jnp.repeat(second_sum, group_width) / cell_count)).astype(jnp.bfloat16)
    time_sum = jnp.stack([jnp.einsum('fhwc,fhwd->cd', extended[2 - k:2 - k + FRAMES].astype(jnp.float32), grad_temporal.astype(jnp.float32)) for k in range(3)])
    grad_ext = jnp.concatenate([grad_temporal, jnp.zeros((2,) + frames.shape[1:], jnp.bfloat16)], 0)
    grad_features = jnp.zeros(frames.shape, jnp.float32)
    for k in range(3):
        grad_features = grad_features + jnp.einsum('fhwd,cd->fhwc', grad_ext[k:k + FRAMES].astype(jnp.float32), time_weight[k].astype(jnp.float32))
    grad_features = grad_features.astype(jnp.bfloat16)
    space_sum = jnp.stack([jnp.stack([jnp.einsum('fhwc,fhwd->cd', padded[:, i:i + HEIGHT, j:j + WIDTH].astype(jnp.float32), grad_features.astype(jnp.float32)) for j in range(3)]) for i in range(3)])
    grad_padded = jnp.pad(grad_features, ((0, 0), (1, 1), (1, 1), (0, 0)))
    grad_input = jnp.zeros(frames.shape, jnp.float32)
    for i in range(3):
        for j in range(3):
            grad_input = grad_input + jnp.einsum('fhwd,cd->fhwc', grad_padded[:, 2 - i:2 - i + HEIGHT, 2 - j:2 - j + WIDTH].astype(jnp.float32), space_weight[i, j].astype(jnp.float32))
    grad_scale = 1.0 / jnp.sqrt(jnp.float32(FRAMES * HEIGHT * WIDTH))
    return (grad_input.astype(jnp.bfloat16), space_sum * grad_scale, time_sum * grad_scale, gain_sum * grad_scale, shift_sum * grad_scale)
```

```python
import jax
import jax.numpy as jnp
from jax import lax
from jax.experimental import pallas as pl
from jax.experimental.pallas import tpu as pltpu
from jax.sharding import PartitionSpec as P

GROUPS = 32


EPSILON = 1e-05
MESH = pl.DeviceIdType.MESH
SIZES = (8, 4, 4)
DEVICES = 128


def everyone():
    here = [lax.axis_index(name) for name in ("tm", "ha", "wa")]
    peers = []
    for a in range(SIZES[0]):
        for b in range(SIZES[1]):
            for c in range(SIZES[2]):
                if (a, b, c) != (0, 0, 0):
                    peers.append(
                        tuple(
                            lax.rem(at + by, size)
                            for at, by, size in zip(here, (a, b, c), SIZES)
                        )
                    )
    return (here[0] * SIZES[1] + here[1]) * SIZES[2] + here[2], peers


def share_kernel(x_ref, out_ref, buf, send_sem, recv_sem):
    me, peers = everyone()
    barrier = pltpu.get_barrier_semaphore()
    for peer in peers:
        pl.semaphore_signal(barrier, inc=1, device_id=peer, device_id_type=MESH)
    buf[me] = x_ref[...]
    pl.semaphore_wait(barrier, DEVICES - 1)
    for peer in peers:
        pltpu.make_async_remote_copy(
            buf.at[me], buf.at[me], send_sem, recv_sem, device_id=peer, device_id_type=MESH
        ).start()
    most = buf.at[pl.ds(0, DEVICES - 1)]
    pltpu.make_async_copy(most, most, recv_sem).wait()
    pltpu.make_async_copy(most, most, send_sem).wait()
    out_ref[...] = buf[...]


def shared(rows, number):
    return pl.pallas_call(
        share_kernel,
        out_shape=jax.ShapeDtypeStruct((DEVICES, 4, 128), jnp.float32),
        in_specs=[pl.BlockSpec(memory_space=pltpu.VMEM)],
        out_specs=pl.BlockSpec(memory_space=pltpu.VMEM),
        scratch_shapes=[
            pltpu.VMEM((DEVICES, 4, 128), jnp.float32),
            pltpu.SemaphoreType.DMA,
            pltpu.SemaphoreType.DMA,
        ],
        compiler_params=pltpu.CompilerParams(collective_id=number, has_side_effects=True),
    )(rows.reshape(4, 128)).reshape(DEVICES, 2, 256)


def padded_2(block, sides, width):
    for axis, dim in sides:
        count = lax.axis_size(axis)
        forward = [(i, i + 1) for i in range(count - 1)]
        backward = [(target, source) for source, target in forward]
        low = lax.ppermute(
            lax.slice_in_dim(block, block.shape[dim] - width, None, axis=dim), axis, forward
        )
        high = lax.ppermute(lax.slice_in_dim(block, 0, width, axis=dim), axis, backward)
        block = jnp.concatenate([low, block, high], axis=dim)
    return block


def passed_along(value, axis, by):
    peers = lax.axis_size(axis)
    pairs = [(i, i + by) for i in range(peers) if 0 <= i + by < peers]
    return lax.ppermute(value, axis, pairs)


def silu_grad(value):
    logistic = jax.nn.sigmoid(value)
    return logistic * (1.0 + value * (1.0 - logistic))


def conv_space(padded, weights, row_count, col_count):
    result = jnp.zeros(padded.shape[:1] + (row_count, col_count, weights.shape[3]), jnp.float32)
    for i in range(3):
        for j in range(3):
            result = result + jnp.einsum(
                "fhwc,cd->fhwd",
                padded[:, i : i + row_count, j : j + col_count],
                weights[i, j],
                preferred_element_type=jnp.float32,
            )
    return result


def group_sum(values, group_width):
    per_channel = jnp.sum(values, axis=(0, 1, 2))
    return per_channel.reshape(-1, group_width).sum(1)


def body(frames, history, cotangent, space_weight, time_weight, norm_gain, norm_shift):
    frame_count, row_count, col_count, channels = frames.shape
    group_width = channels // GROUPS
    all_cells = (
        frame_count
        * row_count
        * col_count
        * lax.axis_size("tm")
        * lax.axis_size("ha")
        * lax.axis_size("wa")
    )
    cell_count = all_cells * group_width
    padded = padded_2(frames, (("ha", 1), ("wa", 2)), 1)
    features = conv_space(padded, space_weight, row_count, col_count).astype(jnp.bfloat16)
    earlier = passed_along(features[frame_count - 2 :], "tm", 1)
    earlier = jnp.where(lax.axis_index("tm") == 0, history, earlier)
    extended = jnp.concatenate([earlier, features], 0)
    temporal = jnp.zeros(frames.shape, jnp.float32)
    for k in range(3):
        temporal = temporal + jnp.einsum(
            "fhwc,cd->fhwd",
            extended[2 - k : 2 - k + frame_count],
            time_weight[k],
            preferred_element_type=jnp.float32,
        )
    local_count = frame_count * row_count * col_count
    mean_local = jnp.sum(temporal, axis=(0, 1, 2)) / local_count
    square_local = jnp.sum(jnp.square(temporal - mean_local), axis=(0, 1, 2))
    parts = shared(jnp.stack([mean_local, square_local]), 0)
    means = parts[:, 0].reshape(DEVICES, GROUPS, group_width)
    mean_value = means.mean((0, 2))
    apart = jnp.sum(jnp.square(means - mean_value[:, None]), axis=(0, 2)) * local_count
    variance = (parts[:, 1].sum(0).reshape(GROUPS, group_width).sum(1) + apart) / cell_count
    centered = temporal - jnp.repeat(mean_value, group_width)
    inv_std = jnp.repeat(lax.rsqrt(variance + EPSILON), group_width)
    normalized = centered * inv_std
    pre_act = normalized * norm_gain + norm_shift
    grad_pre = cotangent.astype(jnp.float32) * silu_grad(pre_act)
    shift_local = jnp.sum(grad_pre, axis=(0, 1, 2))
    gain_local = jnp.sum(grad_pre * normalized, axis=(0, 1, 2))
    grad_norm = grad_pre * norm_gain
    shift_sum, gain_sum = shared(jnp.stack([shift_local, gain_local]), 1).sum(0)
    first_sum = (norm_gain * shift_sum).reshape(GROUPS, group_width).sum(1)
    second_sum = (norm_gain * gain_sum).reshape(GROUPS, group_width).sum(1)
    grad_temporal = (
        inv_std
        * (
            grad_norm
            - jnp.repeat(first_sum, group_width) / cell_count
            - normalized * jnp.repeat(second_sum, group_width) / cell_count
        )
    ).astype(jnp.bfloat16)
    later_grad = passed_along(grad_temporal[:2], "tm", -1)
    grad_ext = jnp.concatenate([grad_temporal, later_grad], 0)
    time_local = jnp.stack(
        [
            jnp.einsum(
                "fhwc,fhwd->cd",
                extended[2 - k : 2 - k + frame_count],
                grad_temporal,
                preferred_element_type=jnp.float32,
            )
            for k in range(3)
        ]
    )
    grad_features = jnp.zeros(frames.shape, jnp.float32)
    for k in range(3):
        grad_features = grad_features + jnp.einsum(
            "fhwd,cd->fhwc",
            grad_ext[k : k + frame_count],
            time_weight[k],
            preferred_element_type=jnp.float32,
        )
    grad_features = grad_features.astype(jnp.bfloat16)
    space_local = jnp.stack(
        [
            jnp.stack(
                [
                    jnp.einsum(
                        "fhwc,fhwd->cd",
                        padded[:, i : i + row_count, j : j + col_count],
                        grad_features,
                        preferred_element_type=jnp.float32,
                    )
                    for j in range(3)
                ]
            )
            for i in range(3)
        ]
    )
    grad_padded = padded_2(grad_features, (("ha", 1), ("wa", 2)), 1)
    grad_input = jnp.zeros(frames.shape, jnp.float32)
    for i in range(3):
        for j in range(3):
            grad_input = grad_input + jnp.einsum(
                "fhwd,cd->fhwc",
                grad_padded[:, 2 - i : 2 - i + row_count, 2 - j : 2 - j + col_count],
                space_weight[i, j],
                preferred_element_type=jnp.float32,
            )
    grad_scale = 1.0 / jnp.sqrt(jnp.float32(all_cells))
    space_sum, time_sum = lax.psum((space_local, time_local), ("tm", "ha", "wa"))
    return (
        grad_input.astype(jnp.bfloat16),
        space_sum * grad_scale,
        time_sum * grad_scale,
        gain_sum * grad_scale,
        shift_sum * grad_scale,
    )


def solution(mesh):
    in_specs = (
        P("tm", "ha", "wa", None),
        P(None, "ha", "wa", None),
        P("tm", "ha", "wa", None),
        P(),
        P(),
        P(),
        P(),
    )
    out_specs = (P("tm", "ha", "wa", None), P(), P(), P(), P())
    return jax.shard_map(body, mesh=mesh, in_specs=in_specs, out_specs=out_specs, check_vma=False)
```

```python
import functools

import jax
import jax.numpy as jnp
from jax import lax
from jax.experimental import pallas as pl
from jax.experimental.pallas import tpu as pltpu
from jax.sharding import PartitionSpec as P

MESH = pl.DeviceIdType.MESH
GROUPS = 32
EPSILON = 1e-05
DEVICES = 128
CHIPS = 64
C = 256
LOCAL = 4096
CELLS = DEVICES * LOCAL
GROUP_CELLS = CELLS * (C // GROUPS)
BF = jnp.bfloat16
F32 = jnp.float32
PIECE = 48
STEPS = ((-1, 0), (1, 0), (0, -1), (0, 1), (-1, -1), (1, -1), (-1, 1), (1, 1))


def dot(a, b):
    return jnp.dot(a, b, preferred_element_type=F32)


def dot_tn(a, b):
    return lax.dot_general(a, b, (((0,), (0,)), ((), ())), preferred_element_type=F32)


def lane_group_sum(x):
    lane = lax.broadcasted_iota(jnp.int32, x.shape, 1)
    for s in (1, 2, 4):
        x = x + jnp.where((lane & s) == 0, pltpu.roll(x, 128 - s, 1), pltpu.roll(x, s, 1))
    return x


def group_sum(row):
    halves = jnp.concatenate([row[:, :128], row[:, 128:], jnp.zeros((6, 128), F32)], axis=0)
    halves = lane_group_sum(halves)
    return jnp.concatenate([halves[0:1], halves[1:2]], axis=1)


def pack_groups(a, b):
    lane = lax.broadcasted_iota(jnp.int32, (1, 128), 1) & 7
    out = jnp.where(lane == 0, a[:, :128], 0.0)
    out = jnp.where(lane == 1, a[:, 128:], out)
    out = jnp.where(lane == 2, b[:, :128], out)
    return jnp.where(lane == 3, b[:, 128:], out)


def unpack_groups(row):
    lane = lax.broadcasted_iota(jnp.int32, (1, 128), 1) & 7
    rows = [jnp.where(lane == k, row, 0.0) for k in range(4)]
    spread = lane_group_sum(jnp.concatenate(rows + [jnp.zeros((4, 128), F32)], axis=0))
    return (
        jnp.concatenate([spread[0:1], spread[1:2]], axis=1),
        jnp.concatenate([spread[2:3], spread[3:4]], axis=1),
    )


def kernel(
    frames, history, cotangent, space_weight, time_weight, gain_ref, shift_ref,
    grad_input, space_out, time_out, param_out,
    x_buf, g_buf, ext, temporal, grad_pre, grad_t, cot, result,
    w_space, w_space_t, w_time, w_time_t,
    edge, halo, acc, sums, stat, chan_y, chan_p,
    core_out, core_in, part, scatter, owned, gathered, gathered_2, final,
    load_sem, store_sem, halo_send, halo_recv, time_send, time_recv,
    back_send, back_recv, stat_send, stat_recv, chan_send, chan_recv,
    core_send, core_recv, big_send, big_recv, last_send, last_recv,
):
    tm, ha, wa = lax.axis_index("tm"), lax.axis_index("ha"), lax.axis_index("wa")
    core = lax.rem(tm, 2)
    me = tm * 16 + ha * 4 + wa
    chip = (tm // 2) * 16 + ha * 4 + wa
    partner = (tm + 1 - 2 * core, ha, wa)
    pending = []

    def device(index):
        return (index // 16, lax.rem(index // 4, 4), lax.rem(index, 4))

    def chip_device(index):
        return (2 * (index // 16) + core, lax.rem(index // 4, 4), lax.rem(index, 4))

    loads = []
    for f in (2, 3, 0, 1):
        rows = pl.ds((f % 2) * 32, 32)
        loads.append(
            pltpu.make_async_copy(
                frames.at[f], x_buf.at[1, f // 2, pl.ds(1, 32), rows], load_sem.at[f]
            )
        )
    loads.append(pltpu.make_async_copy(space_weight, w_space, load_sem.at[4]))
    loads.append(pltpu.make_async_copy(time_weight, w_time, load_sem.at[5]))
    for f in range(4):
        loads.append(
            pltpu.make_async_copy(
                cotangent.at[f], cot.at[f // 2, :, pl.ds((f % 2) * 32, 32)], load_sem.at[6 + f]
            )
        )
    past = [
        pltpu.make_async_copy(history.at[f], ext.at[0, :, pl.ds(f * 32, 32)], load_sem.at[10 + f])
        for f in range(2)
    ]
    for copy in loads:
        copy.start()

    barrier = pltpu.get_barrier_semaphore()

    def greet(i, carry):
        pl.semaphore_signal(
            barrier, inc=1, device_id=device(lax.rem(me + i, DEVICES)), device_id_type=MESH
        )
        return carry

    lax.fori_loop(1, DEVICES, greet, 0)

    @pl.when(tm == 0)
    def _():
        for copy in past:
            copy.start()

    def there(dh, dw):
        ok = None
        for at, by in ((ha, dh), (wa, dw)):
            if by:
                inside = (at + by >= 0) & (at + by <= 3)
                ok = inside if ok is None else ok & inside
        return ok

    def halo_places(kind, p):
        body = (x_buf, g_buf)[kind]
        edges, room = edge.at[kind], halo.at[kind]
        return (
            (body.at[1, p, 1], body.at[1, p, 33]),
            (body.at[1, p, 32], body.at[1, p, 0]),
            (edges.at[0, p], room.at[1, p, pl.ds(16, 64)]),
            (edges.at[1, p], room.at[0, p, pl.ds(16, 64)]),
            (edges.at[0, p, pl.ds(0, 16)], room.at[1, p, pl.ds(80, 16)]),
            (edges.at[0, p, pl.ds(48, 16)], room.at[1, p, pl.ds(0, 16)]),
            (edges.at[1, p, pl.ds(0, 16)], room.at[0, p, pl.ds(80, 16)]),
            (edges.at[1, p, pl.ds(48, 16)], room.at[0, p, pl.ds(0, 16)]),
        )

    def halo_copies(kind, p):
        copies = []
        for n, ((src, dst), (dh, dw)) in enumerate(zip(halo_places(kind, p), STEPS)):
            to = (tm, lax.rem(ha + dh + 4, 4), lax.rem(wa + dw + 4, 4))
            copies.append(
                pltpu.make_async_remote_copy(
                    src, dst, halo_send.at[kind, p, n], halo_recv.at[kind, p, n],
                    device_id=to, device_id_type=MESH,
                )
            )
        return copies

    def halo_zero(kind, p):
        for (_, dst), (dh, dw) in zip(halo_places(kind, p), STEPS):

            @pl.when(jnp.logical_not(there(-dh, -dw)))
            def _():
                dst[...] = jnp.zeros(dst.shape, BF)

    def halo_start(kind, p):
        for copy, (dh, dw) in zip(halo_copies(kind, p), STEPS):
            pl.when(there(dh, dw))(copy.start)

    def halo_wait(kind, p):
        for copy, (dh, dw) in zip(halo_copies(kind, p), STEPS):
            pl.when(there(-dh, -dw))(copy.wait_recv)

    def halo_sent(kind, p):
        for copy, (dh, dw) in zip(halo_copies(kind, p), STEPS):
            pl.when(there(dh, dw))(copy.wait_send)

    row = lax.broadcasted_iota(jnp.int32, (32, 512), 0)
    col = lax.broadcasted_iota(jnp.int32, (32, 512), 1)
    pick = ((row & 15) * 32 + jnp.where(row < 16, 0, 31) == col).astype(F32).astype(BF)

    def take_edges(kind, p):
        body = (x_buf, g_buf)[kind]
        for g in range(4):
            both = dot(pick, body[1, p, 1 + 8 * g : 9 + 8 * g].reshape(512, C)).astype(BF)
            edge[kind, 0, p, 16 * g : 16 * g + 16] = both[:16]
            edge[kind, 1, p, 16 * g : 16 * g + 16] = both[16:]

    place = lax.broadcasted_iota(jnp.int32, (64, C), 0)

    def shift_row(kind, p, h, low, high, v):
        body = (x_buf, g_buf)[kind]
        x = body[1, p, h].astype(F32)
        a = pltpu.roll(x, 1, 0)
        a = jnp.where(place == 0, low[2 * v : 2 * v + 1], a)
        a = jnp.where(place == 32, low[2 * v + 1 : 2 * v + 2], a)
        body[0, p, h] = a.astype(BF)
        b = pltpu.roll(x, 63, 0)
        b = jnp.where(place == 31, high[2 * v : 2 * v + 1], b)
        b = jnp.where(place == 63, high[2 * v + 1 : 2 * v + 2], b)
        body[2, p, h] = b.astype(BF)

    def shift_all(kind, p):
        for h, at, v in ((0, 0, 7), (33, 80, 0)):
            low = halo[kind, 0, p, at : at + 16].astype(F32)
            high = halo[kind, 1, p, at : at + 16].astype(F32)
            shift_row(kind, p, h, low, high, v)

        @pl.loop(0, 4)
        def _(g):
            at = pl.ds(pl.multiple_of(16 * g + 16, 16), 16)
            low = halo[kind, 0, p, at].astype(F32)
            high = halo[kind, 1, p, at].astype(F32)
            for v in range(8):
                shift_row(kind, p, 8 * g + 1 + v, low, high, v)

    def conv(kind, p, h, count, weights):
        body = (x_buf, g_buf)[kind]
        lhs = jnp.concatenate(
            [
                body[j, p, pl.ds(h + i, count)].reshape(count * 64, C)
                for i in range(3)
                for j in range(3)
            ],
            axis=1,
        )
        return dot(lhs, weights[...]).astype(BF).reshape(count, 64, C)

    for kind in range(2):
        for p in range(2):
            halo_zero(kind, p)

    @pl.when(tm == 7)
    def _():
        grad_t[2] = jnp.zeros((32, 64, C), BF)

    loads[0].wait()
    loads[1].wait()
    take_edges(0, 1)
    loads[2].wait()
    loads[3].wait()
    take_edges(0, 0)
    pl.semaphore_wait(barrier, DEVICES - 1)
    halo_start(0, 1)
    halo_start(0, 0)
    loads[4].wait()
    loads[5].wait()
    for t in range(9):
        w_space_t[t * C : (t + 1) * C] = w_space[(8 - t) * C : (9 - t) * C].T
    for k in range(3):
        w_time_t[k * C : (k + 1) * C] = w_time[k * C : (k + 1) * C].T

    def to_next(n):
        part_rows = pl.ds(n * 8, 8)
        return pltpu.make_async_remote_copy(
            ext.at[2, part_rows], ext.at[0, part_rows], time_send.at[n], time_recv.at[n],
            device_id=(lax.rem(tm + 1, 8), ha, wa), device_id_type=MESH,
        )

    halo_wait(0, 1)
    shift_all(0, 1)
    for n in range(4):
        ext[2, 8 * n : 8 * n + 8] = conv(0, 1, 8 * n, 8, w_space)
        pl.when(tm < 7)(to_next(n).start)
    halo_wait(0, 0)
    shift_all(0, 0)
    for n in range(2):
        ext[1, 16 * n : 16 * n + 16] = conv(0, 0, 16 * n, 16, w_space)

    def between(a, b):
        return jnp.concatenate([a[:, 32:], b[:, :32]], axis=1)

    def temporal_pair(q):
        sums[0:1] = jnp.zeros((1, C), F32)

        @pl.loop(0, 2)
        def _(n):
            s = pl.ds(n * 16, 16)
            a, b = ext[q, s], ext[q + 1, s]
            lhs = jnp.concatenate(
                [v.reshape(1024, C) for v in (b, between(a, b), a)], axis=1
            )
            t = dot(lhs, w_time[...])
            temporal[q, s] = t.reshape(16, 64, C)
            sums[0:1] += jnp.sum(t, axis=0, keepdims=True)

        mean = group_sum(sums[0:1]) * (1.0 / (2048 * 8))
        sums[1:2] = jnp.zeros((1, C), F32)

        @pl.loop(0, 8)
        def _(n):
            apart = temporal[q, pl.ds(n * 4, 4)].reshape(256, C) - mean
            sums[1:2] += jnp.sum(apart * apart, axis=0, keepdims=True)

        return mean, group_sum(sums[1:2])

    mean_1, square_1 = temporal_pair(1)
    pl.when(tm == 0)(past[0].wait)
    pl.when(tm == 0)(past[1].wait)
    for n in range(4):
        pl.when(tm > 0)(to_next(n).wait_recv)
    mean_0, square_0 = temporal_pair(0)
    mean_here = 0.5 * (mean_0 + mean_1)
    square_here = square_0 + square_1 + (0.5 * 2048 * 8) * jnp.square(mean_0 - mean_1)

    def share_start(n, packed):
        stat[n, me] = packed

        def send(i, carry):
            pltpu.make_async_remote_copy(
                stat.at[n, me], stat.at[n, me], stat_send.at[n], stat_recv.at[n],
                device_id=device(lax.rem(me + i, DEVICES)), device_id_type=MESH,
            ).start()
            return carry

        lax.fori_loop(1, DEVICES, send, 0)

    def share_wait(n, sem):
        most = stat.at[n, pl.ds(0, DEVICES - 1)]
        pltpu.make_async_copy(most, most, sem.at[n]).wait()

    share_start(0, pack_groups(mean_here, square_here))
    share_wait(0, stat_recv)
    all_stat = stat[0]
    average = jnp.sum(all_stat, axis=0) * (1.0 / DEVICES)
    total = jnp.sum(all_stat, axis=0)
    spread = jnp.sum(jnp.square(all_stat - average), axis=0) * (LOCAL * 8.0)
    mean, spread = unpack_groups(average)[0], unpack_groups(spread)[0]
    variance = (unpack_groups(total)[1] + spread) * (1.0 / GROUP_CELLS)
    inv_std = lax.rsqrt(variance + EPSILON)
    gain, norm_shift = gain_ref[...], shift_ref[...]

    for copy in loads[6:]:
        copy.wait()
    sums[2:4] = jnp.zeros((2, C), F32)
    for q in range(2):

        @pl.loop(0, 16)
        def _(n):
            s = pl.ds(n * 2, 2)
            normal = (temporal[q, s].reshape(128, C) - mean) * inv_std
            value = normal * gain + norm_shift
            logistic = 0.5 + 0.5 * jnp.tanh(0.5 * value)
            slope = logistic * (1.0 + value * (1.0 - logistic))
            g = cot[q, s].reshape(128, C).astype(F32) * slope
            temporal[q, s] = normal.reshape(2, 64, C)
            grad_pre[q, s] = g.reshape(2, 64, C)
            sums[2:3] += jnp.sum(g, axis=0, keepdims=True)
            sums[3:4] += jnp.sum(g * normal, axis=0, keepdims=True)

    shift_here, gain_here = sums[2:3], sums[3:4]
    share_start(1, pack_groups(group_sum(gain * shift_here), group_sum(gain * gain_here)))

    chan_here = jnp.concatenate(
        [shift_here[:, :128], shift_here[:, 128:], gain_here[:, :128], gain_here[:, 128:]], axis=0
    )

    def chan_copy(step, i):
        if step == 0:
            return pltpu.make_async_remote_copy(
                chan_y.at[tm], chan_y.at[tm], chan_send.at[0], chan_recv.at[0],
                device_id=(lax.rem(tm + i, 8), ha, wa), device_id_type=MESH,
            )
        at = ha * 4 + wa
        to = lax.rem(at + i, 16)
        return pltpu.make_async_remote_copy(
            chan_p.at[at], chan_p.at[at], chan_send.at[1], chan_recv.at[1],
            device_id=(tm, to // 4, lax.rem(to, 4)), device_id_type=MESH,
        )

    def chan_start(step, value):
        if step == 0:
            chan_y[tm] = value
        else:
            chan_p[ha * 4 + wa] = value
        for i in range(1, (8, 16)[step]):
            chan_copy(step, i).start()

    def chan_wait(step, sem):
        most = (chan_y, chan_p)[step].at[pl.ds(0, (7, 15)[step])]
        pltpu.make_async_copy(most, most, sem.at[step]).wait()

    chan_start(0, chan_here)
    share_wait(1, stat_recv)
    first, second = unpack_groups(jnp.sum(stat[1], axis=0))
    scale_g = inv_std * gain
    offset = inv_std * first * (1.0 / GROUP_CELLS)
    scale_n = inv_std * second * (1.0 / GROUP_CELLS)

    def to_previous(n):
        part_rows = pl.ds(n * 8, 8)
        return pltpu.make_async_remote_copy(
            grad_t.at[0, part_rows], grad_t.at[2, part_rows], back_send.at[n], back_recv.at[n],
            device_id=(lax.rem(tm + 7, 8), ha, wa), device_id_type=MESH,
        )

    for q in range(2):
        for n in range(4):
            for half in range(2):
                s = pl.ds(n * 8 + half * 4, 4)
                g = grad_pre[q, s].reshape(256, C) * scale_g - offset
                g = g - temporal[q, s].reshape(256, C) * scale_n
                grad_t[q, s] = g.astype(BF).reshape(4, 64, C)
            if q == 0:
                pl.when(tm > 0)(to_previous(n).start)

    for k in range(3):
        total_k = None
        for q in range(2):
            for n in range(2):
                s = slice(n * 16, n * 16 + 16)
                if k == 0:
                    e = ext[q + 1, s]
                elif k == 1:
                    e = between(ext[q, s], ext[q + 1, s])
                else:
                    e = ext[q, s]
                d = dot_tn(e.reshape(1024, C), grad_t[q, s].reshape(1024, C))
                total_k = d if total_k is None else total_k + d
        acc[0, 9 + k] = total_k[:, :128]
        acc[1, 9 + k] = total_k[:, 128:]

    chan_wait(0, chan_recv)
    chan_start(1, jnp.sum(chan_y[...], axis=0))

    def features_back(p):
        @pl.loop(0, 2)
        def _(n):
            s = pl.ds(n * 16, 16)
            a, b = grad_t[p, s], grad_t[p + 1, s]
            lhs = jnp.concatenate(
                [v.reshape(1024, C) for v in (a, between(a, b), b)], axis=1
            )
            g_buf[1, p, pl.ds(n * 16 + 1, 16)] = (
                dot(lhs, w_time_t[...]).astype(BF).reshape(16, 64, C)
            )

        take_edges(1, p)
        halo_start(1, p)

    def space_tap(p, t):
        i, j = t // 3, lax.rem(t, 3)
        return dot_tn(
            x_buf[j, p, pl.ds(i, 32)].reshape(2048, C), g_buf[1, p, 1:33].reshape(2048, C)
        )

    stores = [
        pltpu.make_async_copy(
            result.at[f // 2, :, pl.ds((f % 2) * 32, 32)], grad_input.at[f], store_sem.at[f]
        )
        for f in range(4)
    ]

    def input_back(p):
        halo_wait(1, p)
        shift_all(1, p)
        for n in range(2):
            result[p, 16 * n : 16 * n + 16] = conv(1, p, 16 * n, 16, w_space_t)
        stores[2 * p].start()
        stores[2 * p + 1].start()

    def core_copy(t):
        return pltpu.make_async_remote_copy(
            core_out.at[t], core_in.at[t], core_send.at[t], core_recv.at[t],
            device_id=partner, device_id_type=MESH,
        )

    def core_start(t):
        core_out[t] = acc[1 - core, t].astype(BF)
        core_copy(t).start()

    features_back(0)

    @pl.loop(0, 9)
    def _(t):
        d = space_tap(0, t)
        acc[0, t] = d[:, :128]
        acc[1, t] = d[:, 128:]

    for t in range(9, 12):
        core_start(t)
    input_back(0)
    for n in range(4):
        pl.when(tm < 7)(to_previous(n).wait_recv)
    features_back(1)

    @pl.loop(0, 9)
    def _(t):
        d = space_tap(1, t)
        acc[0, t] += d[:, :128]
        acc[1, t] += d[:, 128:]
        core_start(t)

    @pl.loop(0, 12)
    def _(t):
        core_copy(t).wait_recv()
        part[pl.ds(pl.multiple_of(t * 256, 256), 256)] = (
            acc[core, t] + core_in[t].astype(F32)
        ).astype(BF)

    def rows_of(index):
        return pl.ds(pl.multiple_of(index * PIECE, PIECE), PIECE)

    def scatter_start(i, carry):
        to = lax.rem(chip + i, CHIPS)
        pltpu.make_async_remote_copy(
            part.at[rows_of(to)], scatter.at[chip], big_send.at[0], big_recv.at[0],
            device_id=chip_device(to), device_id_type=MESH,
        ).start()
        return carry

    lax.fori_loop(1, CHIPS, scatter_start, 0)
    scatter[chip] = part[rows_of(chip)]
    input_back(1)

    def big_wait(buf, sem, n):
        most = buf.at[pl.ds(0, CHIPS - 1)]
        pltpu.make_async_copy(most, most, sem.at[n]).wait()

    big_wait(scatter, big_recv, 0)
    owned[...] = jnp.sum(scatter[...].astype(F32), axis=0).astype(BF)

    def gather_start(i, carry):
        pltpu.make_async_remote_copy(
            owned, gathered.at[chip], big_send.at[1], big_recv.at[1],
            device_id=chip_device(lax.rem(chip + i, CHIPS)), device_id_type=MESH,
        ).start()
        return carry

    lax.fori_loop(1, CHIPS, gather_start, 0)
    gathered[chip] = owned[...]

    grad_scale = float(CELLS) ** -0.5
    chan_wait(1, chan_recv)
    param_out[...] = jnp.sum(chan_p[...], axis=0) * grad_scale

    big_wait(gathered, big_recv, 1)
    swap = pltpu.make_async_remote_copy(
        gathered, gathered_2, last_send, last_recv, device_id=partner, device_id_type=MESH
    )
    swap.start()

    def put(source, half):
        whole = source[...].reshape(12, 256, 128)
        final[:, :, pl.ds(pl.multiple_of(half * 128, 128), 128)] = whole.astype(F32) * grad_scale

    put(gathered, core)
    swap.wait_recv()
    put(gathered_2, 1 - core)
    ends = [
        pltpu.make_async_copy(final.at[pl.ds(0, 9)], space_out, store_sem.at[4]),
        pltpu.make_async_copy(final.at[pl.ds(9, 3)], time_out, store_sem.at[5]),
    ]
    for copy in ends:
        copy.start()

    for kind in range(2):
        for p in range(2):
            halo_sent(kind, p)
    for n in range(4):
        pl.when(tm < 7)(to_next(n).wait_send)
        pl.when(tm > 0)(to_previous(n).wait_send)
    share_wait(0, stat_send)
    share_wait(1, stat_send)
    chan_wait(0, chan_send)
    chan_wait(1, chan_send)

    @pl.loop(0, 12)
    def _(t):
        core_copy(t).wait_send()

    big_wait(scatter, big_send, 0)
    big_wait(gathered, big_send, 1)
    swap.wait_send()
    for copy in stores + ends:
        copy.wait()


def body(frames, history, cotangent, space_weight, time_weight, norm_gain, norm_shift):
    hbm = pl.BlockSpec(memory_space=pl.ANY)
    vmem = pl.BlockSpec(memory_space=pltpu.VMEM)
    dma = pltpu.SemaphoreType.DMA
    grad_input, space_grad, time_grad, params = pl.pallas_call(
        kernel,
        out_shape=(
            jax.ShapeDtypeStruct((4, 32, 32, C), BF),
            jax.ShapeDtypeStruct((9, C, C), F32),
            jax.ShapeDtypeStruct((3, C, C), F32),
            jax.ShapeDtypeStruct((4, 128), F32),
        ),
        in_specs=[hbm] * 5 + [vmem] * 2,
        out_specs=(hbm, hbm, hbm, vmem),
        scratch_shapes=[
            pltpu.VMEM((3, 2, 34, 64, C), BF),
            pltpu.VMEM((3, 2, 34, 64, C), BF),
            pltpu.VMEM((3, 32, 64, C), BF),
            pltpu.VMEM((2, 32, 64, C), F32),
            pltpu.VMEM((2, 32, 64, C), F32),
            pltpu.VMEM((3, 32, 64, C), BF),
            pltpu.VMEM((2, 32, 64, C), BF),
            pltpu.VMEM((2, 32, 64, C), BF),
            pltpu.VMEM((9 * C, C), BF),
            pltpu.VMEM((9 * C, C), BF),
            pltpu.VMEM((3 * C, C), BF),
            pltpu.VMEM((3 * C, C), BF),
            pltpu.VMEM((2, 2, 2, 64, C), BF),
            pltpu.VMEM((2, 2, 2, 96, C), BF),
            pltpu.VMEM((2, 12, C, 128), F32),
            pltpu.VMEM((8, C), F32),
            pltpu.VMEM((2, DEVICES, 1, 128), F32),
            pltpu.VMEM((8, 4, 128), F32),
            pltpu.VMEM((16, 4, 128), F32),
            pltpu.VMEM((12, C, 128), BF),
            pltpu.VMEM((12, C, 128), BF),
            pltpu.VMEM((12 * C, 128), BF),
            pltpu.VMEM((CHIPS, PIECE, 128), BF),
            pltpu.VMEM((PIECE, 128), BF),
            pltpu.VMEM((CHIPS, PIECE, 128), BF),
            pltpu.VMEM((CHIPS, PIECE, 128), BF),
            pltpu.VMEM((12, C, C), F32),
            dma((12,)),
            dma((6,)),
            dma((2, 2, 8)),
            dma((2, 2, 8)),
            dma((4,)),
            dma((4,)),
            dma((4,)),
            dma((4,)),
            dma((2,)),
            dma((2,)),
            dma((2,)),
            dma((2,)),
            dma((12,)),
            dma((12,)),
            dma((2,)),
            dma((2,)),
            dma,
            dma,
        ],
        compiler_params=pltpu.CompilerParams(
            collective_id=0, has_side_effects=True, vmem_limit_bytes=58 << 20
        ),
        name="decoder_block_backward",
    )(
        frames,
        history,
        cotangent,
        space_weight.reshape(9 * C, C),
        time_weight.reshape(3 * C, C),
        norm_gain.reshape(1, C),
        norm_shift.reshape(1, C),
    )
    params = params.reshape(2, C)
    return grad_input, space_grad.reshape(3, 3, C, C), time_grad, params[1], params[0]


def solution(mesh):
    split = P("tm", "ha", "wa", None)
    in_specs = (split, P(None, "ha", "wa", None), split, P(), P(), P(), P())
    out_specs = (split, P(), P(), P(), P())
    return jax.shard_map(body, mesh=mesh, in_specs=in_specs, out_specs=out_specs, check_vma=False)
```

```python
import functools

import jax
import jax.numpy as jnp
from jax import lax
from jax.experimental import pallas as pl
from jax.experimental.pallas import tpu as pltpu
from jax.sharding import PartitionSpec as P

MESH = pl.DeviceIdType.MESH
GROUPS = 32
EPSILON = 1e-05
DEVICES = 128
CHIPS = 64
C = 256
LOCAL = 4096
CELLS = DEVICES * LOCAL
GROUP_CELLS = CELLS * (C // GROUPS)
BF = jnp.bfloat16
F32 = jnp.float32
PIECE = 48
STEPS = ((-1, 0), (1, 0), (0, -1), (0, 1), (-1, -1), (1, -1), (-1, 1), (1, 1))


def far_first(offsets):
    def hops(offset):
        t, h, w = offset
        most = max(o[0] for o in offsets) + 1
        chips = (t + 1) // 2 if most == 8 else t
        return sum(min(n, 4 - n) for n in (chips % 4, h, w))

    return sorted(offsets[1:], key=hops, reverse=True)


def dot(a, b):
    return jnp.dot(a, b, preferred_element_type=F32)


def dot_tn(a, b):
    return lax.dot_general(a, b, (((0,), (0,)), ((), ())), preferred_element_type=F32)


def lane_group_sum(x):
    lane = lax.broadcasted_iota(jnp.int32, x.shape, 1)
    for s in (1, 2, 4):
        x = x + jnp.where((lane & s) == 0, pltpu.roll(x, 128 - s, 1), pltpu.roll(x, s, 1))
    return x


def group_sum(row):
    halves = jnp.concatenate([row[:, :128], row[:, 128:], jnp.zeros((6, 128), F32)], axis=0)
    halves = lane_group_sum(halves)
    return jnp.concatenate([halves[0:1], halves[1:2]], axis=1)


def pack_groups(a, b):
    lane = lax.broadcasted_iota(jnp.int32, (1, 128), 1) & 7
    out = jnp.where(lane == 0, a[:, :128], 0.0)
    out = jnp.where(lane == 1, a[:, 128:], out)
    out = jnp.where(lane == 2, b[:, :128], out)
    return jnp.where(lane == 3, b[:, 128:], out)


def unpack_groups(row):
    lane = lax.broadcasted_iota(jnp.int32, (1, 128), 1) & 7
    rows = [jnp.where(lane == k, row, 0.0) for k in range(4)]
    spread = lane_group_sum(jnp.concatenate(rows + [jnp.zeros((4, 128), F32)], axis=0))
    return (
        jnp.concatenate([spread[0:1], spread[1:2]], axis=1),
        jnp.concatenate([spread[2:3], spread[3:4]], axis=1),
    )


def kernel(
    frames, history, cotangent, space_weight, time_weight, gain_ref, shift_ref,
    grad_input, half_out, other_out, param_out,
    x_buf, x_past, g_buf, g_part, ext, temporal, grad_pre, grad_t, cot, result,
    w_space, w_space_t, w_time, w_time_t,
    edge, halo, halo_past, acc, sums, stat, chan_y, chan_p,
    core_out, core_in, part, scatter, plane_sum, column_part, owned, gathered, gathered_2,
    load_sem, store_sem, past_send, past_recv, halo_send, halo_recv, time_send, time_recv,
    back_send, back_recv, stat_send, stat_recv, chan_send, chan_recv,
    core_send, core_recv, big_send, big_recv, column_recv, down_recv, gather_recv, last_send, last_recv, all_here,
):
    tm, ha, wa = lax.axis_index("tm"), lax.axis_index("ha"), lax.axis_index("wa")
    core = lax.rem(tm, 2)
    height = lax.div(tm, 2)
    me = tm * 16 + ha * 4 + wa
    partner = (tm + 1 - 2 * core, ha, wa)
    spot = ha * 4 + wa
    frame_ring = [lax.rem(tm + n, 8) for n in range(8)]
    heights = [lax.rem(height + n, 4) for n in range(4)]
    rows_ring = [lax.rem(ha + n, 4) for n in range(4)]
    cols_ring = [lax.rem(wa + n, 4) for n in range(4)]
    column = [(t, ha, wa) for t in frame_ring[1:]]
    plane = [(tm, h, w) for h in rows_ring for w in cols_ring][1:]
    everyone = [
        (frame_ring[t], rows_ring[h], cols_ring[w])
        for t, h, w in far_first([(t, h, w) for t in range(8) for h in range(4) for w in range(4)])
    ]
    others = [(2 * y + core, ha, wa) for y in heights[1:]]
    around = [
        (rows_ring[h], cols_ring[w])
        for _, h, w in far_first([(0, h, w) for h in range(4) for w in range(4)])
    ]

    loads = []
    for f in (2, 3, 0, 1):
        rows = pl.ds((f % 2) * 32, 32)
        loads.append(
            pltpu.make_async_copy(
                frames.at[f], x_buf.at[1, f // 2, pl.ds(1, 32), rows], load_sem.at[f]
            )
        )
    loads.append(pltpu.make_async_copy(space_weight, w_space, load_sem.at[4]))
    loads.append(pltpu.make_async_copy(time_weight, w_time, load_sem.at[5]))
    for f in range(4):
        loads.append(
            pltpu.make_async_copy(
                cotangent.at[f], cot.at[f // 2, :, pl.ds((f % 2) * 32, 32)], load_sem.at[6 + f]
            )
        )
    past = [
        pltpu.make_async_copy(history.at[f], ext.at[0, :, pl.ds(f * 32, 32)], load_sem.at[10 + f])
        for f in range(2)
    ]
    for copy in loads:
        copy.start()

    barrier = pltpu.get_barrier_semaphore()

    for peer in column + plane:
        pl.semaphore_signal(barrier, inc=1, device_id=peer, device_id_type=MESH)

    @pl.when(tm == 0)
    def _():
        for copy in past:
            copy.start()

    def there(dh, dw):
        ok = None
        for at, by in ((ha, dh), (wa, dw)):
            if by:
                inside = (at + by >= 0) & (at + by <= 3)
                ok = inside if ok is None else ok & inside
        return ok

    def halo_places(kind, p):
        body = (x_buf, g_buf)[kind]
        edges, room = edge.at[kind], halo.at[kind]
        return (
            (body.at[1, p, 1], body.at[1, p, 33]),
            (body.at[1, p, 32], body.at[1, p, 0]),
            (edges.at[0, p], room.at[1, p, pl.ds(16, 64)]),
            (edges.at[1, p], room.at[0, p, pl.ds(16, 64)]),
            (edges.at[0, p, pl.ds(0, 16)], room.at[1, p, pl.ds(80, 16)]),
            (edges.at[0, p, pl.ds(48, 16)], room.at[1, p, pl.ds(0, 16)]),
            (edges.at[1, p, pl.ds(0, 16)], room.at[0, p, pl.ds(80, 16)]),
            (edges.at[1, p, pl.ds(48, 16)], room.at[0, p, pl.ds(0, 16)]),
        )

    def halo_copies(kind, p):
        copies = []
        for n, ((src, dst), (dh, dw)) in enumerate(zip(halo_places(kind, p), STEPS)):
            to = (tm, lax.rem(ha + dh + 4, 4), lax.rem(wa + dw + 4, 4))
            copies.append(
                pltpu.make_async_remote_copy(
                    src, dst, halo_send.at[kind, p, n], halo_recv.at[kind, p, n],
                    device_id=to, device_id_type=MESH,
                )
            )
        return copies

    def halo_zero(kind, p):
        for (_, dst), (dh, dw) in zip(halo_places(kind, p), STEPS):

            @pl.when(jnp.logical_not(there(-dh, -dw)))
            def _():
                dst[...] = jnp.zeros(dst.shape, BF)

    def halo_start(kind, p):
        for copy, (dh, dw) in zip(halo_copies(kind, p), STEPS):
            pl.when(there(dh, dw))(copy.start)

    def halo_wait(kind, p):
        for copy, (dh, dw) in zip(halo_copies(kind, p), STEPS):
            pl.when(there(-dh, -dw))(copy.wait_recv)

    def halo_sent(kind, p):
        for copy, (dh, dw) in zip(halo_copies(kind, p), STEPS):
            pl.when(there(dh, dw))(copy.wait_send)

    row = lax.broadcasted_iota(jnp.int32, (32, 512), 0)
    col = lax.broadcasted_iota(jnp.int32, (32, 512), 1)
    pick = ((row & 15) * 32 + jnp.where(row < 16, 0, 31) == col).astype(F32).astype(BF)

    def take_edges(kind, p):
        body = (x_buf, g_buf)[kind]
        for g in range(4):
            both = dot(pick, body[1, p, 1 + 8 * g : 9 + 8 * g].reshape(512, C)).astype(BF)
            edge[kind, 0, p, 16 * g : 16 * g + 16] = both[:16]
            edge[kind, 1, p, 16 * g : 16 * g + 16] = both[16:]

    place = lax.broadcasted_iota(jnp.int32, (64, C), 0)

    def shift_row(body, h, low, high, v):
        x = body[1, h].astype(F32)
        a = pltpu.roll(x, 1, 0)
        a = jnp.where(place == 0, low[2 * v : 2 * v + 1], a)
        a = jnp.where(place == 32, low[2 * v + 1 : 2 * v + 2], a)
        body[0, h] = a.astype(BF)
        b = pltpu.roll(x, 63, 0)
        b = jnp.where(place == 31, high[2 * v : 2 * v + 1], b)
        b = jnp.where(place == 63, high[2 * v + 1 : 2 * v + 2], b)
        body[2, h] = b.astype(BF)

    def shift_all(body, room):
        for h, at, v in ((0, 0, 7), (33, 80, 0)):
            low = room[0, at : at + 16].astype(F32)
            high = room[1, at : at + 16].astype(F32)
            shift_row(body, h, low, high, v)

        @pl.loop(0, 4)
        def _(g):
            at = pl.ds(pl.multiple_of(16 * g + 16, 16), 16)
            low = room[0, at].astype(F32)
            high = room[1, at].astype(F32)
            for v in range(8):
                shift_row(body, 8 * g + 1 + v, low, high, v)

    def conv(kind, p, h, count, weights):
        body = (x_buf, g_buf)[kind]
        lhs = jnp.concatenate(
            [
                body[j, p, pl.ds(h + i, count)].reshape(count * 64, C)
                for i in range(3)
                for j in range(3)
            ],
            axis=1,
        )
        return dot(lhs, weights[...]).astype(BF).reshape(count, 64, C)

    for kind in range(2):
        for p in range(2):
            halo_zero(kind, p)

    @pl.when(tm == 7)
    def _():
        grad_t[2] = jnp.zeros((32, 64, C), BF)

    @pl.when(tm == 0)
    def _():
        x_past[...] = jnp.zeros(x_past.shape, BF)

    loads[0].wait()
    loads[1].wait()
    take_edges(0, 1)
    loads[2].wait()
    loads[3].wait()
    take_edges(0, 0)
    pl.semaphore_wait(barrier, len(column + plane))
    for peer in column:
        pl.semaphore_signal(all_here, inc=1, device_id=peer, device_id_type=MESH)
    halo_start(0, 1)
    halo_start(0, 0)
    loads[4].wait()
    loads[5].wait()
    for t in range(9):
        w_space_t[t * C : (t + 1) * C] = w_space[(8 - t) * C : (9 - t) * C].T
    for k in range(3):
        w_time_t[k * C : (k + 1) * C] = w_time[k * C : (k + 1) * C].T

    def to_next(n):
        part_rows = pl.ds(n * 8, 8)
        return pltpu.make_async_remote_copy(
            ext.at[2, part_rows], ext.at[0, part_rows], time_send.at[n], time_recv.at[n],
            device_id=(lax.rem(tm + 1, 8), ha, wa), device_id_type=MESH,
        )

    halo_wait(0, 1)
    shift_all(x_buf.at[:, 1], halo.at[0, :, 1])
    for n in range(4):
        ext[2, 8 * n : 8 * n + 8] = conv(0, 1, 8 * n, 8, w_space)
        pl.when(tm < 7)(to_next(n).start)
    halo_wait(0, 0)
    shift_all(x_buf.at[:, 0], halo.at[0, :, 0])
    for n in range(2):
        ext[1, 16 * n : 16 * n + 16] = conv(0, 0, 16 * n, 16, w_space)

    def between(a, b):
        return jnp.concatenate([a[:, 32:], b[:, :32]], axis=1)

    def temporal_pair(q):
        sums[0:1] = jnp.zeros((1, C), F32)

        @pl.loop(0, 2)
        def _(n):
            s = pl.ds(n * 16, 16)
            a, b = ext[q, s], ext[q + 1, s]
            lhs = jnp.concatenate(
                [v.reshape(1024, C) for v in (b, between(a, b), a)], axis=1
            )
            t = dot(lhs, w_time[...])
            temporal[q, s] = t.reshape(16, 64, C)
            sums[0:1] += jnp.sum(t, axis=0, keepdims=True)

        mean = group_sum(sums[0:1]) * (1.0 / (2048 * 8))
        sums[1:2] = jnp.zeros((1, C), F32)

        @pl.loop(0, 8)
        def _(n):
            apart = temporal[q, pl.ds(n * 4, 4)].reshape(256, C) - mean
            sums[1:2] += jnp.sum(apart * apart, axis=0, keepdims=True)

        return mean, group_sum(sums[1:2])

    mean_1, square_1 = temporal_pair(1)
    pl.when(tm == 0)(past[0].wait)
    pl.when(tm == 0)(past[1].wait)
    for n in range(4):
        pl.when(tm > 0)(to_next(n).wait_recv)
    mean_0, square_0 = temporal_pair(0)
    mean_here = 0.5 * (mean_0 + mean_1)
    square_here = square_0 + square_1 + (0.5 * 2048 * 8) * jnp.square(mean_0 - mean_1)

    def share_start(n, packed):
        stat[n, me] = packed

        for peer in everyone:
            pltpu.make_async_remote_copy(
                stat.at[n, me], stat.at[n, me], stat_send.at[n], stat_recv.at[n],
                device_id=peer, device_id_type=MESH,
            ).start()

    def share_wait(n, sem):
        most = stat.at[n, pl.ds(0, DEVICES - 1)]
        pltpu.make_async_copy(most, most, sem.at[n]).wait()

    ahead = (lax.rem(tm + 1, 8), ha, wa)
    frames_on = [
        pltpu.make_async_remote_copy(
            src, dst, past_send.at[n], past_recv.at[n], device_id=ahead, device_id_type=MESH
        )
        for n, (src, dst) in enumerate(
            ((x_buf.at[1, 1], x_past.at[1]), (halo.at[0, :, 1], halo_past))
        )
    ]
    pl.semaphore_wait(all_here, len(column))
    share_start(0, pack_groups(mean_here, square_here))
    for copy in frames_on:
        pl.when(tm < 7)(copy.start)
    share_wait(0, stat_recv)
    all_stat = stat[0]
    average = jnp.sum(all_stat, axis=0) * (1.0 / DEVICES)
    total = jnp.sum(all_stat, axis=0)
    spread = jnp.sum(jnp.square(all_stat - average), axis=0) * (LOCAL * 8.0)
    mean, spread = unpack_groups(average)[0], unpack_groups(spread)[0]
    variance = (unpack_groups(total)[1] + spread) * (1.0 / GROUP_CELLS)
    inv_std = lax.rsqrt(variance + EPSILON)
    gain, norm_shift = gain_ref[...], shift_ref[...]

    for copy in loads[6:]:
        copy.wait()
    sums[2:4] = jnp.zeros((2, C), F32)
    for q in range(2):

        @pl.loop(0, 16)
        def _(n):
            s = pl.ds(n * 2, 2)
            normal = (temporal[q, s].reshape(128, C) - mean) * inv_std
            value = normal * gain + norm_shift
            logistic = 0.5 + 0.5 * jnp.tanh(0.5 * value)
            slope = logistic * (1.0 + value * (1.0 - logistic))
            g = cot[q, s].reshape(128, C).astype(F32) * slope
            temporal[q, s] = normal.reshape(2, 64, C)
            grad_pre[q, s] = g.reshape(2, 64, C)
            sums[2:3] += jnp.sum(g, axis=0, keepdims=True)
            sums[3:4] += jnp.sum(g * normal, axis=0, keepdims=True)

    shift_here, gain_here = sums[2:3], sums[3:4]
    share_start(1, pack_groups(group_sum(gain * shift_here), group_sum(gain * gain_here)))

    chan_here = jnp.concatenate(
        [shift_here[:, :128], shift_here[:, 128:], gain_here[:, :128], gain_here[:, 128:]], axis=0
    )

    def chan_copy(step, i):
        if step == 0:
            return pltpu.make_async_remote_copy(
                chan_y.at[tm], chan_y.at[tm], chan_send.at[0], chan_recv.at[0],
                device_id=column[i - 1], device_id_type=MESH,
            )
        at = ha * 4 + wa
        return pltpu.make_async_remote_copy(
            chan_p.at[at], chan_p.at[at], chan_send.at[1], chan_recv.at[1],
            device_id=plane[i - 1], device_id_type=MESH,
        )

    def chan_start(step, value):
        if step == 0:
            chan_y[tm] = value
        else:
            chan_p[ha * 4 + wa] = value
        for i in range(1, (8, 16)[step]):
            chan_copy(step, i).start()

    def chan_wait(step, sem):
        most = (chan_y, chan_p)[step].at[pl.ds(0, (7, 15)[step])]
        pltpu.make_async_copy(most, most, sem.at[step]).wait()

    chan_start(0, chan_here)

    @pl.when(tm > 0)
    def _():
        for copy in frames_on:
            copy.wait_recv()
        shift_all(x_past, halo_past)

    share_wait(1, stat_recv)
    first, second = unpack_groups(jnp.sum(stat[1], axis=0))
    scale_g = inv_std * gain
    offset = inv_std * first * (1.0 / GROUP_CELLS)
    scale_n = inv_std * second * (1.0 / GROUP_CELLS)

    def to_previous(n):
        part_rows = pl.ds(n * 8, 8)
        return pltpu.make_async_remote_copy(
            grad_t.at[0, part_rows], grad_t.at[2, part_rows], back_send.at[n], back_recv.at[n],
            device_id=(lax.rem(tm + 7, 8), ha, wa), device_id_type=MESH,
        )

    for q in range(2):
        for n in range(4):
            for half in range(2):
                s = pl.ds(n * 8 + half * 4, 4)
                g = grad_pre[q, s].reshape(256, C) * scale_g - offset
                g = g - temporal[q, s].reshape(256, C) * scale_n
                grad_t[q, s] = g.astype(BF).reshape(4, 64, C)
            if q == 0:
                pl.when(tm > 0)(to_previous(n).start)

    for k in range(3):
        total_k = None
        for q in range(2):
            for n in range(2):
                s = slice(n * 16, n * 16 + 16)
                if k == 0:
                    e = ext[q + 1, s]
                elif k == 1:
                    e = between(ext[q, s], ext[q + 1, s])
                else:
                    e = ext[q, s]
                d = dot_tn(e.reshape(1024, C), grad_t[q, s].reshape(1024, C))
                total_k = d if total_k is None else total_k + d
        acc[0, 9 + k] = total_k[:, :128]
        acc[1, 9 + k] = total_k[:, 128:]

    chan_wait(0, chan_recv)
    chan_start(1, jnp.sum(chan_y[...], axis=0))

    def features_back(p):
        @pl.loop(0, 2)
        def _(n):
            s = pl.ds(n * 16, 16)
            a, b = grad_t[p, s], grad_t[p + 1, s]
            lhs = jnp.concatenate(
                [v.reshape(1024, C) for v in (a, between(a, b), b)], axis=1
            )
            g_buf[1, p, pl.ds(n * 16 + 1, 16)] = (
                dot(lhs, w_time_t[...]).astype(BF).reshape(16, 64, C)
            )

        take_edges(1, p)
        halo_start(1, p)

    def features_parts():
        @pl.loop(0, 2)
        def _(n):
            s = pl.ds(n * 16, 16)
            a, b = grad_t[1, s], grad_t[0, s]
            none = jnp.zeros((16, 32, C), BF)
            for m, (lhs, rhs) in enumerate(
                (
                    ((a, jnp.concatenate([a[:, 32:], none], axis=1)), w_time_t[: 2 * C]),
                    ((jnp.concatenate([none, b[:, :32]], axis=1), b), w_time_t[C:]),
                )
            ):
                lhs = jnp.concatenate([v.reshape(1024, C) for v in lhs], axis=1)
                g_part[m, s] = dot(lhs, rhs).astype(BF).reshape(16, 64, C)

    def space_tap(t):
        i, j = t // 3, lax.rem(t, 3)
        rows = pl.ds(i, 32)
        pairs = (
            (x_buf[j, 0, rows], g_buf[1, 0, 1:33]),
            (x_buf[j, 1, rows], g_part[0]),
            (x_past[j, rows], g_part[1]),
        )
        return sum(dot_tn(x.reshape(2048, C), g.reshape(2048, C)) for x, g in pairs)

    stores = [
        pltpu.make_async_copy(
            result.at[f // 2, :, pl.ds((f % 2) * 32, 32)], grad_input.at[f], store_sem.at[f]
        )
        for f in range(4)
    ]

    def input_back(p):
        halo_wait(1, p)
        shift_all(g_buf.at[:, p], halo.at[1, :, p])
        for n in range(2):
            result[p, 16 * n : 16 * n + 16] = conv(1, p, 16 * n, 16, w_space_t)
        stores[2 * p].start()
        stores[2 * p + 1].start()

    def core_copy(t):
        return pltpu.make_async_remote_copy(
            core_out.at[t], core_in.at[t], core_send.at[t], core_recv.at[t],
            device_id=partner, device_id_type=MESH,
        )

    def core_start(t):
        core_out[t] = acc[1 - core, t].astype(BF)
        core_copy(t).start()

    def rows_of(index):
        return pl.ds(pl.multiple_of(index * PIECE, PIECE), PIECE)

    def core_sum(group):
        for t in range(3 * group, 3 * group + 3):
            core_copy(t).wait_recv()
            part[t * 256 : t * 256 + 256] = (acc[core, t] + core_in[t].astype(F32)).astype(BF)

    def scatter_start(group):
        core_sum(group)
        for h, w in around:
            pltpu.make_async_remote_copy(
                part.at[rows_of(group * 16 + h * 4 + w)], scatter.at[group * 16 + spot],
                big_send.at[0], big_recv.at[group],
                device_id=(tm, h, w), device_id_type=MESH,
            ).start()
        scatter[group * 16 + spot] = part[rows_of(group * 16 + spot)]

    def big_wait(buf, sem, count):
        most = buf.at[pl.ds(0, count)]
        pltpu.make_async_copy(most, most, sem).wait()

    def up_copy(group):
        return pltpu.make_async_remote_copy(
            plane_sum.at[group], column_part.at[height], big_send.at[1], column_recv.at[0],
            device_id=(2 * group + core, ha, wa), device_id_type=MESH,
        )

    def add_plane(group):
        big_wait(scatter, big_recv.at[group], 15)
        rows = scatter[16 * group : 16 * group + 16].astype(F32)
        plane_sum[group] = jnp.sum(rows, axis=0).astype(BF)

        @pl.when(height == group)
        def _():
            column_part[group] = plane_sum[group]

        pl.when(height != group)(up_copy(group).start)

    def down_copy(to):
        return pltpu.make_async_remote_copy(
            owned, gathered.at[height * 16 + spot], big_send.at[2], down_recv.at[height],
            device_id=to, device_id_type=MESH,
        )

    def add_column():
        big_wait(column_part, column_recv.at[0], 3)
        owned[...] = jnp.sum(column_part[...].astype(F32), axis=0).astype(BF)
        for to in others:
            down_copy(to).start()
        gathered[height * 16 + spot] = owned[...]

    def spread(group):
        place_here = gathered.at[group * 16 + spot]

        @pl.when(height != group)
        def _():
            pltpu.make_async_copy(place_here, place_here, down_recv.at[group]).wait()

        for h, w in around:
            pltpu.make_async_remote_copy(
                place_here, place_here, big_send.at[3], gather_recv.at[group],
                device_id=(tm, h, w), device_id_type=MESH,
            ).start()

    def swap_copy(group):
        span = pl.ds(group * 16, 16)
        return pltpu.make_async_remote_copy(
            gathered.at[span], gathered_2.at[span], last_send.at[group], last_recv.at[group],
            device_id=partner, device_id_type=MESH,
        )

    def keep_copies(group):
        span = pl.ds(group * 16, 16)
        return (
            pltpu.make_async_copy(gathered.at[span], half_out.at[span], store_sem.at[4 + group]),
            pltpu.make_async_copy(gathered_2.at[span], other_out.at[span], store_sem.at[8 + group]),
        )

    def taps(low, high):
        @pl.loop(low, high)
        def _(t):
            d = space_tap(t)
            acc[0, t] = d[:, :128]
            acc[1, t] = d[:, 128:]
            core_start(t)

    for t in range(9, 12):
        core_start(t)
    features_back(0)
    features_parts()

    scatter_start(3)
    taps(0, 4)
    scatter_start(0)
    add_plane(3)
    taps(4, 7)
    scatter_start(1)
    add_plane(0)
    taps(7, 9)
    for n in range(4):
        pl.when(tm < 7)(to_previous(n).wait_recv)
    features_back(1)
    scatter_start(2)
    pl.when((height == 3) | (height == 0))(add_column)
    add_plane(1)
    input_back(0)
    add_plane(2)
    pl.when(height == 1)(add_column)
    spread(3)
    spread(0)
    input_back(1)
    pl.when(height == 2)(add_column)
    spread(1)
    spread(2)

    grad_scale = float(CELLS) ** -0.5
    chan_wait(1, chan_recv)
    param_out[...] = jnp.sum(chan_p[...], axis=0) * grad_scale

    for group in (3, 0, 1, 2):
        big_wait(gathered, gather_recv.at[group], 15)
        swap_copy(group).start()
        keep_copies(group)[0].start()
    for group in (3, 0, 1, 2):
        swap_copy(group).wait_recv()
        keep_copies(group)[1].start()

    for kind in range(2):
        for p in range(2):
            halo_sent(kind, p)
    for n in range(4):
        pl.when(tm < 7)(to_next(n).wait_send)
        pl.when(tm > 0)(to_previous(n).wait_send)
    for copy in frames_on:
        pl.when(tm < 7)(copy.wait_send)
    share_wait(0, stat_send)
    share_wait(1, stat_send)
    chan_wait(0, chan_send)
    chan_wait(1, chan_send)

    @pl.loop(0, 12)
    def _(t):
        core_copy(t).wait_send()

    big_wait(scatter, big_send.at[0], 60)
    big_wait(plane_sum, big_send.at[1], 3)
    big_wait(plane_sum, big_send.at[2], 3)
    big_wait(gathered, big_send.at[3], 60)
    for group in range(4):
        swap_copy(group).wait_send()
        for copy in keep_copies(group):
            copy.wait()
    for copy in stores:
        copy.wait()


def finish(
    grad_in, half, other, params, grad_input, space_out, time_out, gain_out, shift_out
):
    core = lax.rem(lax.axis_index("tm"), 2)
    step = pl.program_id(0)
    grad_scale = float(CELLS) ** -0.5
    grad_input[...] = grad_in[...]
    shift_out[...] = jnp.concatenate([params[0:1], params[1:2]], axis=1)
    gain_out[...] = jnp.concatenate([params[2:3], params[3:4]], axis=1)

    def put(out):
        a = half[...].reshape(3, C, 128).astype(F32) * grad_scale
        b = other[...].reshape(3, C, 128).astype(F32) * grad_scale
        out[:, :, :128] = jnp.where(core == 0, a, b)
        out[:, :, 128:] = jnp.where(core == 0, b, a)

    pl.when(step < 3)(functools.partial(put, space_out))
    pl.when(step == 3)(functools.partial(put, time_out))


def body(frames, history, cotangent, space_weight, time_weight, norm_gain, norm_shift):
    hbm = pl.BlockSpec(memory_space=pl.ANY)
    vmem = pl.BlockSpec(memory_space=pltpu.VMEM)
    dma = pltpu.SemaphoreType.DMA
    chunks = jax.ShapeDtypeStruct((CHIPS, PIECE, 128), BF)
    grad_input, half, other, params = pl.pallas_call(
        kernel,
        out_shape=(
            jax.ShapeDtypeStruct((4, 32, 32, C), BF),
            chunks,
            chunks,
            jax.ShapeDtypeStruct((4, 128), F32),
        ),
        in_specs=[hbm] * 5 + [vmem] * 2,
        out_specs=(hbm, hbm, hbm, vmem),
        scratch_shapes=[
            pltpu.VMEM((3, 2, 34, 64, C), BF),
            pltpu.VMEM((3, 34, 64, C), BF),
            pltpu.VMEM((3, 2, 34, 64, C), BF),
            pltpu.VMEM((2, 32, 64, C), BF),
            pltpu.VMEM((3, 32, 64, C), BF),
            pltpu.VMEM((2, 32, 64, C), F32),
            pltpu.VMEM((2, 32, 64, C), F32),
            pltpu.VMEM((3, 32, 64, C), BF),
            pltpu.VMEM((2, 32, 64, C), BF),
            pltpu.VMEM((2, 32, 64, C), BF),
            pltpu.VMEM((9 * C, C), BF),
            pltpu.VMEM((9 * C, C), BF),
            pltpu.VMEM((3 * C, C), BF),
            pltpu.VMEM((3 * C, C), BF),
            pltpu.VMEM((2, 2, 2, 64, C), BF),
            pltpu.VMEM((2, 2, 2, 96, C), BF),
            pltpu.VMEM((2, 96, C), BF),
            pltpu.VMEM((2, 12, C, 128), F32),
            pltpu.VMEM((8, C), F32),
            pltpu.VMEM((2, DEVICES, 1, 128), F32),
            pltpu.VMEM((8, 4, 128), F32),
            pltpu.VMEM((16, 4, 128), F32),
            pltpu.VMEM((12, C, 128), BF),
            pltpu.VMEM((12, C, 128), BF),
            pltpu.VMEM((12 * C, 128), BF),
            pltpu.VMEM((CHIPS, PIECE, 128), BF),
            pltpu.VMEM((4, PIECE, 128), BF),
            pltpu.VMEM((4, PIECE, 128), BF),
            pltpu.VMEM((PIECE, 128), BF),
            pltpu.VMEM((CHIPS, PIECE, 128), BF),
            pltpu.VMEM((CHIPS, PIECE, 128), BF),
            dma((12,)),
            dma((12,)),
            dma((2,)),
            dma((2,)),
            dma((2, 2, 8)),
            dma((2, 2, 8)),
            dma((4,)),
            dma((4,)),
            dma((4,)),
            dma((4,)),
            dma((2,)),
            dma((2,)),
            dma((2,)),
            dma((2,)),
            dma((12,)),
            dma((12,)),
            dma((4,)),
            dma((4,)),
            dma((1,)),
            dma((4,)),
            dma((4,)),
            dma((4,)),
            dma((4,)),
            pltpu.SemaphoreType.REGULAR,
        ],
        compiler_params=pltpu.CompilerParams(
            collective_id=0, has_side_effects=True, vmem_limit_bytes=58 << 20
        ),
        name="decoder_block_backward",
    )(
        frames,
        history,
        cotangent,
        space_weight.reshape(9 * C, C),
        time_weight.reshape(3 * C, C),
        norm_gain.reshape(1, C),
        norm_shift.reshape(1, C),
    )
    grad_input, space_grad, time_grad, gain_grad, shift_grad = pl.pallas_call(
        finish,
        out_shape=(
            jax.ShapeDtypeStruct((4, 32, 32, C), BF),
            jax.ShapeDtypeStruct((9, C, C), F32),
            jax.ShapeDtypeStruct((3, C, C), F32),
            jax.ShapeDtypeStruct((1, C), F32),
            jax.ShapeDtypeStruct((1, C), F32),
        ),
        grid=(4,),
        in_specs=[
            pl.BlockSpec((1, 32, 32, C), lambda n: (n, 0, 0, 0)),
            pl.BlockSpec((16, PIECE, 128), lambda n: (n, 0, 0)),
            pl.BlockSpec((16, PIECE, 128), lambda n: (n, 0, 0)),
            pl.BlockSpec((4, 128), lambda n: (0, 0)),
        ],
        out_specs=(
            pl.BlockSpec((1, 32, 32, C), lambda n: (n, 0, 0, 0)),
            pl.BlockSpec((3, C, C), lambda n: (jnp.minimum(n, 2), 0, 0)),
            pl.BlockSpec((3, C, C), lambda n: (0, 0, 0)),
            pl.BlockSpec((1, C), lambda n: (0, 0)),
            pl.BlockSpec((1, C), lambda n: (0, 0)),
        ),
        compiler_params=pltpu.CompilerParams(vmem_limit_bytes=58 << 20),
        name="scale_and_store",
    )(grad_input, half, other, params)
    return (
        grad_input,
        space_grad.reshape(3, 3, C, C),
        time_grad,
        gain_grad.reshape(C),
        shift_grad.reshape(C),
    )


def solution(mesh):
    split = P("tm", "ha", "wa", None)
    in_specs = (split, P(None, "ha", "wa", None), split, P(), P(), P(), P())
    out_specs = (split, P(), P(), P(), P())
    return jax.shard_map(body, mesh=mesh, in_specs=in_specs, out_specs=out_specs, check_vma=False)
```

```python
import functools

import jax
import jax.numpy as jnp
from jax import lax
from jax.experimental import pallas as pl
from jax.experimental.pallas import tpu as pltpu
from jax.sharding import PartitionSpec as P

MESH = pl.DeviceIdType.MESH
GROUPS = 32
EPSILON = 1e-05
DEVICES = 128
CHIPS = 64
C = 256
LOCAL = 4096
CELLS = DEVICES * LOCAL
GROUP_CELLS = CELLS * (C // GROUPS)
BF = jnp.bfloat16
F32 = jnp.float32
PIECE = 48
STEPS = ((-1, 0), (1, 0), (0, -1), (0, 1), (-1, -1), (1, -1), (-1, 1), (1, 1))


def far_first(offsets):
    def hops(offset):
        t, h, w = offset
        most = max(o[0] for o in offsets) + 1
        chips = (t + 1) // 2 if most == 8 else t
        return sum(min(n, 4 - n) for n in (chips % 4, h, w))

    return sorted(offsets[1:], key=hops, reverse=True)


def dot(a, b):
    return jnp.dot(a, b, preferred_element_type=F32)


def dot_tn(a, b):
    return lax.dot_general(a, b, (((0,), (0,)), ((), ())), preferred_element_type=F32)


def lane_group_sum(x):
    lane = lax.broadcasted_iota(jnp.int32, x.shape, 1)
    for s in (1, 2, 4):
        x = x + jnp.where((lane & s) == 0, pltpu.roll(x, 128 - s, 1), pltpu.roll(x, s, 1))
    return x


def group_sum(row):
    halves = jnp.concatenate([row[:, :128], row[:, 128:], jnp.zeros((6, 128), F32)], axis=0)
    halves = lane_group_sum(halves)
    return jnp.concatenate([halves[0:1], halves[1:2]], axis=1)


def pack_groups(a, b):
    lane = lax.broadcasted_iota(jnp.int32, (1, 128), 1) & 7
    out = jnp.where(lane == 0, a[:, :128], 0.0)
    out = jnp.where(lane == 1, a[:, 128:], out)
    out = jnp.where(lane == 2, b[:, :128], out)
    return jnp.where(lane == 3, b[:, 128:], out)


def unpack_groups(row):
    lane = lax.broadcasted_iota(jnp.int32, (1, 128), 1) & 7
    rows = [jnp.where(lane == k, row, 0.0) for k in range(4)]
    spread = lane_group_sum(jnp.concatenate(rows + [jnp.zeros((4, 128), F32)], axis=0))
    return (
        jnp.concatenate([spread[0:1], spread[1:2]], axis=1),
        jnp.concatenate([spread[2:3], spread[3:4]], axis=1),
    )


def kernel(
    frames, history, cotangent, space_weight, time_weight, gain_ref, shift_ref,
    grad_input, half_out, other_out, param_out,
    x_buf, x_past, g_buf, g_part, ext, temporal, grad_pre, grad_t, cot, result,
    w_space, w_space_t, w_time, w_time_t,
    edge, halo, halo_past, acc, sums, stat, chan_y, chan_p,
    core_out, core_in, part, scatter, plane_sum, column_part, gathered, gathered_2,
    load_sem, store_sem, past_send, past_recv, halo_send, halo_recv, time_send, time_recv,
    back_send, back_recv, stat_send, stat_recv, chan_send, chan_recv,
    core_send, core_recv, big_send, big_recv, column_recv, gather_recv, last_send, last_recv, all_here,
):
    tm, ha, wa = lax.axis_index("tm"), lax.axis_index("ha"), lax.axis_index("wa")
    core = lax.rem(tm, 2)
    height = lax.div(tm, 2)
    me = tm * 16 + ha * 4 + wa
    partner = (tm + 1 - 2 * core, ha, wa)
    spot = ha * 4 + wa
    frame_ring = [lax.rem(tm + n, 8) for n in range(8)]
    heights = [lax.rem(height + n, 4) for n in range(4)]
    rows_ring = [lax.rem(ha + n, 4) for n in range(4)]
    cols_ring = [lax.rem(wa + n, 4) for n in range(4)]
    column = [(t, ha, wa) for t in frame_ring[1:]]
    plane = [(tm, h, w) for h in rows_ring for w in cols_ring][1:]
    everyone = [
        (frame_ring[t], rows_ring[h], cols_ring[w])
        for t, h, w in far_first([(t, h, w) for t in range(8) for h in range(4) for w in range(4)])
    ]
    others = [(2 * y + core, ha, wa) for y in heights[1:]]
    around = [
        (rows_ring[h], cols_ring[w])
        for _, h, w in far_first([(0, h, w) for h in range(4) for w in range(4)])
    ]

    loads = []
    for f in (2, 3, 0, 1):
        rows = pl.ds((f % 2) * 32, 32)
        loads.append(
            pltpu.make_async_copy(
                frames.at[f], x_buf.at[1, f // 2, pl.ds(1, 32), rows], load_sem.at[f]
            )
        )
    loads.append(pltpu.make_async_copy(space_weight, w_space, load_sem.at[4]))
    loads.append(pltpu.make_async_copy(time_weight, w_time, load_sem.at[5]))
    for f in range(4):
        loads.append(
            pltpu.make_async_copy(
                cotangent.at[f], cot.at[f // 2, :, pl.ds((f % 2) * 32, 32)], load_sem.at[6 + f]
            )
        )
    past = [
        pltpu.make_async_copy(history.at[f], ext.at[0, :, pl.ds(f * 32, 32)], load_sem.at[10 + f])
        for f in range(2)
    ]
    for copy in loads:
        copy.start()

    barrier = pltpu.get_barrier_semaphore()

    for peer in column + plane:
        pl.semaphore_signal(barrier, inc=1, device_id=peer, device_id_type=MESH)

    @pl.when(tm == 0)
    def _():
        for copy in past:
            copy.start()

    def there(dh, dw):
        ok = None
        for at, by in ((ha, dh), (wa, dw)):
            if by:
                inside = (at + by >= 0) & (at + by <= 3)
                ok = inside if ok is None else ok & inside
        return ok

    def halo_places(kind, p):
        body = (x_buf, g_buf)[kind]
        edges, room = edge.at[kind], halo.at[kind]
        return (
            (body.at[1, p, 1], body.at[1, p, 33]),
            (body.at[1, p, 32], body.at[1, p, 0]),
            (edges.at[0, p], room.at[1, p, pl.ds(16, 64)]),
            (edges.at[1, p], room.at[0, p, pl.ds(16, 64)]),
            (edges.at[0, p, pl.ds(0, 16)], room.at[1, p, pl.ds(80, 16)]),
            (edges.at[0, p, pl.ds(48, 16)], room.at[1, p, pl.ds(0, 16)]),
            (edges.at[1, p, pl.ds(0, 16)], room.at[0, p, pl.ds(80, 16)]),
            (edges.at[1, p, pl.ds(48, 16)], room.at[0, p, pl.ds(0, 16)]),
        )

    def halo_copies(kind, p):
        copies = []
        for n, ((src, dst), (dh, dw)) in enumerate(zip(halo_places(kind, p), STEPS)):
            to = (tm, lax.rem(ha + dh + 4, 4), lax.rem(wa + dw + 4, 4))
            copies.append(
                pltpu.make_async_remote_copy(
                    src, dst, halo_send.at[kind, p, n], halo_recv.at[kind, p, n],
                    device_id=to, device_id_type=MESH,
                )
            )
        return copies

    def halo_zero(kind, p):
        for (_, dst), (dh, dw) in zip(halo_places(kind, p), STEPS):

            @pl.when(jnp.logical_not(there(-dh, -dw)))
            def _():
                dst[...] = jnp.zeros(dst.shape, BF)

    def halo_start(kind, p):
        for copy, (dh, dw) in zip(halo_copies(kind, p), STEPS):
            pl.when(there(dh, dw))(copy.start)

    def halo_wait(kind, p):
        for copy, (dh, dw) in zip(halo_copies(kind, p), STEPS):
            pl.when(there(-dh, -dw))(copy.wait_recv)

    def halo_sent(kind, p):
        for copy, (dh, dw) in zip(halo_copies(kind, p), STEPS):
            pl.when(there(dh, dw))(copy.wait_send)

    row = lax.broadcasted_iota(jnp.int32, (32, 512), 0)
    col = lax.broadcasted_iota(jnp.int32, (32, 512), 1)
    pick = ((row & 15) * 32 + jnp.where(row < 16, 0, 31) == col).astype(F32).astype(BF)

    def take_edges(kind, p):
        body = (x_buf, g_buf)[kind]
        for g in range(4):
            both = dot(pick, body[1, p, 1 + 8 * g : 9 + 8 * g].reshape(512, C)).astype(BF)
            edge[kind, 0, p, 16 * g : 16 * g + 16] = both[:16]
            edge[kind, 1, p, 16 * g : 16 * g + 16] = both[16:]

    place = lax.broadcasted_iota(jnp.int32, (64, C), 0)

    def shift_row(body, h, low, high, v):
        x = body[1, h].astype(F32)
        a = pltpu.roll(x, 1, 0)
        a = jnp.where(place == 0, low[2 * v : 2 * v + 1], a)
        a = jnp.where(place == 32, low[2 * v + 1 : 2 * v + 2], a)
        body[0, h] = a.astype(BF)
        b = pltpu.roll(x, 63, 0)
        b = jnp.where(place == 31, high[2 * v : 2 * v + 1], b)
        b = jnp.where(place == 63, high[2 * v + 1 : 2 * v + 2], b)
        body[2, h] = b.astype(BF)

    def shift_all(body, room):
        for h, at, v in ((0, 0, 7), (33, 80, 0)):
            low = room[0, at : at + 16].astype(F32)
            high = room[1, at : at + 16].astype(F32)
            shift_row(body, h, low, high, v)

        @pl.loop(0, 4)
        def _(g):
            at = pl.ds(pl.multiple_of(16 * g + 16, 16), 16)
            low = room[0, at].astype(F32)
            high = room[1, at].astype(F32)
            for v in range(8):
                shift_row(body, 8 * g + 1 + v, low, high, v)

    def conv(kind, p, h, count, weights):
        body = (x_buf, g_buf)[kind]
        lhs = jnp.concatenate(
            [
                body[j, p, pl.ds(h + i, count)].reshape(count * 64, C)
                for i in range(3)
                for j in range(3)
            ],
            axis=1,
        )
        return dot(lhs, weights[...]).astype(BF).reshape(count, 64, C)

    for kind in range(2):
        for p in range(2):
            halo_zero(kind, p)

    @pl.when(tm == 7)
    def _():
        grad_t[2] = jnp.zeros((32, 64, C), BF)

    @pl.when(tm == 0)
    def _():
        x_past[...] = jnp.zeros(x_past.shape, BF)

    loads[0].wait()
    loads[1].wait()
    take_edges(0, 1)
    loads[2].wait()
    loads[3].wait()
    take_edges(0, 0)
    pl.semaphore_wait(barrier, len(column + plane))
    for peer in column:
        pl.semaphore_signal(all_here, inc=1, device_id=peer, device_id_type=MESH)
    halo_start(0, 1)
    halo_start(0, 0)
    loads[4].wait()
    loads[5].wait()
    for t in range(9):
        w_space_t[t * C : (t + 1) * C] = w_space[(8 - t) * C : (9 - t) * C].T
    for k in range(3):
        w_time_t[k * C : (k + 1) * C] = w_time[k * C : (k + 1) * C].T

    def to_next(n):
        part_rows = pl.ds(n * 8, 8)
        return pltpu.make_async_remote_copy(
            ext.at[2, part_rows], ext.at[0, part_rows], time_send.at[n], time_recv.at[n],
            device_id=(lax.rem(tm + 1, 8), ha, wa), device_id_type=MESH,
        )

    halo_wait(0, 1)
    shift_all(x_buf.at[:, 1], halo.at[0, :, 1])
    for n in range(4):
        ext[2, 8 * n : 8 * n + 8] = conv(0, 1, 8 * n, 8, w_space)
        pl.when(tm < 7)(to_next(n).start)
    halo_wait(0, 0)
    shift_all(x_buf.at[:, 0], halo.at[0, :, 0])
    for n in range(2):
        ext[1, 16 * n : 16 * n + 16] = conv(0, 0, 16 * n, 16, w_space)

    def between(a, b):
        return jnp.concatenate([a[:, 32:], b[:, :32]], axis=1)

    def temporal_pair(q):
        sums[0:1] = jnp.zeros((1, C), F32)

        @pl.loop(0, 2)
        def _(n):
            s = pl.ds(n * 16, 16)
            a, b = ext[q, s], ext[q + 1, s]
            lhs = jnp.concatenate(
                [v.reshape(1024, C) for v in (b, between(a, b), a)], axis=1
            )
            t = dot(lhs, w_time[...])
            temporal[q, s] = t.reshape(16, 64, C)
            sums[0:1] += jnp.sum(t, axis=0, keepdims=True)

        mean = group_sum(sums[0:1]) * (1.0 / (2048 * 8))
        sums[1:2] = jnp.zeros((1, C), F32)

        @pl.loop(0, 8)
        def _(n):
            apart = temporal[q, pl.ds(n * 4, 4)].reshape(256, C) - mean
            sums[1:2] += jnp.sum(apart * apart, axis=0, keepdims=True)

        return mean, group_sum(sums[1:2])

    mean_1, square_1 = temporal_pair(1)
    pl.when(tm == 0)(past[0].wait)
    pl.when(tm == 0)(past[1].wait)
    for n in range(4):
        pl.when(tm > 0)(to_next(n).wait_recv)
    mean_0, square_0 = temporal_pair(0)
    mean_here = 0.5 * (mean_0 + mean_1)
    square_here = square_0 + square_1 + (0.5 * 2048 * 8) * jnp.square(mean_0 - mean_1)

    def share_start(n, packed):
        stat[n, me] = packed

        for peer in everyone:
            pltpu.make_async_remote_copy(
                stat.at[n, me], stat.at[n, me], stat_send.at[n], stat_recv.at[n],
                device_id=peer, device_id_type=MESH,
            ).start()

    def share_wait(n, sem):
        most = stat.at[n, pl.ds(0, DEVICES - 1)]
        pltpu.make_async_copy(most, most, sem.at[n]).wait()

    ahead = (lax.rem(tm + 1, 8), ha, wa)
    frames_on = [
        pltpu.make_async_remote_copy(
            src, dst, past_send.at[n], past_recv.at[n], device_id=ahead, device_id_type=MESH
        )
        for n, (src, dst) in enumerate(
            ((x_buf.at[1, 1], x_past.at[1]), (halo.at[0, :, 1], halo_past))
        )
    ]
    pl.semaphore_wait(all_here, len(column))
    share_start(0, pack_groups(mean_here, square_here))
    for copy in frames_on:
        pl.when(tm < 7)(copy.start)
    share_wait(0, stat_recv)
    all_stat = stat[0]
    average = jnp.sum(all_stat, axis=0) * (1.0 / DEVICES)
    total = jnp.sum(all_stat, axis=0)
    spread = jnp.sum(jnp.square(all_stat - average), axis=0) * (LOCAL * 8.0)
    mean, spread = unpack_groups(average)[0], unpack_groups(spread)[0]
    variance = (unpack_groups(total)[1] + spread) * (1.0 / GROUP_CELLS)
    inv_std = lax.rsqrt(variance + EPSILON)
    gain, norm_shift = gain_ref[...], shift_ref[...]

    for copy in loads[6:]:
        copy.wait()
    sums[2:4] = jnp.zeros((2, C), F32)
    for q in range(2):

        @pl.loop(0, 16)
        def _(n):
            s = pl.ds(n * 2, 2)
            normal = (temporal[q, s].reshape(128, C) - mean) * inv_std
            value = normal * gain + norm_shift
            logistic = 0.5 + 0.5 * jnp.tanh(0.5 * value)
            slope = logistic * (1.0 + value * (1.0 - logistic))
            g = cot[q, s].reshape(128, C).astype(F32) * slope
            temporal[q, s] = normal.reshape(2, 64, C)
            grad_pre[q, s] = g.reshape(2, 64, C)
            sums[2:3] += jnp.sum(g, axis=0, keepdims=True)
            sums[3:4] += jnp.sum(g * normal, axis=0, keepdims=True)

    shift_here, gain_here = sums[2:3], sums[3:4]
    share_start(1, pack_groups(group_sum(gain * shift_here), group_sum(gain * gain_here)))

    chan_here = jnp.concatenate(
        [shift_here[:, :128], shift_here[:, 128:], gain_here[:, :128], gain_here[:, 128:]], axis=0
    )

    def chan_copy(step, i):
        if step == 0:
            return pltpu.make_async_remote_copy(
                chan_y.at[tm], chan_y.at[tm], chan_send.at[0], chan_recv.at[0],
                device_id=column[i - 1], device_id_type=MESH,
            )
        at = ha * 4 + wa
        return pltpu.make_async_remote_copy(
            chan_p.at[at], chan_p.at[at], chan_send.at[1], chan_recv.at[1],
            device_id=plane[i - 1], device_id_type=MESH,
        )

    def chan_start(step, value):
        if step == 0:
            chan_y[tm] = value
        else:
            chan_p[ha * 4 + wa] = value
        for i in range(1, (8, 16)[step]):
            chan_copy(step, i).start()

    def chan_wait(step, sem):
        most = (chan_y, chan_p)[step].at[pl.ds(0, (7, 15)[step])]
        pltpu.make_async_copy(most, most, sem.at[step]).wait()

    chan_start(0, chan_here)

    @pl.when(tm > 0)
    def _():
        for copy in frames_on:
            copy.wait_recv()
        shift_all(x_past, halo_past)

    share_wait(1, stat_recv)
    first, second = unpack_groups(jnp.sum(stat[1], axis=0))
    scale_g = inv_std * gain
    offset = inv_std * first * (1.0 / GROUP_CELLS)
    scale_n = inv_std * second * (1.0 / GROUP_CELLS)

    def to_previous(n):
        part_rows = pl.ds(n * 8, 8)
        return pltpu.make_async_remote_copy(
            grad_t.at[0, part_rows], grad_t.at[2, part_rows], back_send.at[n], back_recv.at[n],
            device_id=(lax.rem(tm + 7, 8), ha, wa), device_id_type=MESH,
        )

    for q in range(2):
        for n in range(4):
            for half in range(2):
                s = pl.ds(n * 8 + half * 4, 4)
                g = grad_pre[q, s].reshape(256, C) * scale_g - offset
                g = g - temporal[q, s].reshape(256, C) * scale_n
                grad_t[q, s] = g.astype(BF).reshape(4, 64, C)
            if q == 0:
                pl.when(tm > 0)(to_previous(n).start)

    for k in range(3):
        total_k = None
        for q in range(2):
            for n in range(2):
                s = slice(n * 16, n * 16 + 16)
                if k == 0:
                    e = ext[q + 1, s]
                elif k == 1:
                    e = between(ext[q, s], ext[q + 1, s])
                else:
                    e = ext[q, s]
                d = dot_tn(e.reshape(1024, C), grad_t[q, s].reshape(1024, C))
                total_k = d if total_k is None else total_k + d
        acc[0, 9 + k] = total_k[:, :128]
        acc[1, 9 + k] = total_k[:, 128:]

    chan_wait(0, chan_recv)
    chan_start(1, jnp.sum(chan_y[...], axis=0))

    def features_back(p):
        @pl.loop(0, 2)
        def _(n):
            s = pl.ds(n * 16, 16)
            a, b = grad_t[p, s], grad_t[p + 1, s]
            lhs = jnp.concatenate(
                [v.reshape(1024, C) for v in (a, between(a, b), b)], axis=1
            )
            g_buf[1, p, pl.ds(n * 16 + 1, 16)] = (
                dot(lhs, w_time_t[...]).astype(BF).reshape(16, 64, C)
            )

        take_edges(1, p)
        halo_start(1, p)

    def features_parts():
        @pl.loop(0, 2)
        def _(n):
            s = pl.ds(n * 16, 16)
            a, b = grad_t[1, s], grad_t[0, s]
            none = jnp.zeros((16, 32, C), BF)
            for m, (lhs, rhs) in enumerate(
                (
                    ((a, jnp.concatenate([a[:, 32:], none], axis=1)), w_time_t[: 2 * C]),
                    ((jnp.concatenate([none, b[:, :32]], axis=1), b), w_time_t[C:]),
                )
            ):
                lhs = jnp.concatenate([v.reshape(1024, C) for v in lhs], axis=1)
                g_part[m, s] = dot(lhs, rhs).astype(BF).reshape(16, 64, C)

    def space_tap(t):
        i, j = t // 3, lax.rem(t, 3)
        rows = pl.ds(i, 32)
        pairs = (
            (x_buf[j, 0, rows], g_buf[1, 0, 1:33]),
            (x_buf[j, 1, rows], g_part[0]),
            (x_past[j, rows], g_part[1]),
        )
        return sum(dot_tn(x.reshape(2048, C), g.reshape(2048, C)) for x, g in pairs)

    stores = [
        pltpu.make_async_copy(
            result.at[f // 2, :, pl.ds((f % 2) * 32, 32)], grad_input.at[f], store_sem.at[f]
        )
        for f in range(4)
    ]

    def input_back(p, halfway=None):
        halo_wait(1, p)
        shift_all(g_buf.at[:, p], halo.at[1, :, p])
        for n in range(2):
            result[p, 16 * n : 16 * n + 16] = conv(1, p, 16 * n, 16, w_space_t)
            if n == 0 and halfway is not None:
                halfway()
        stores[2 * p].start()
        stores[2 * p + 1].start()

    def core_copy(t):
        return pltpu.make_async_remote_copy(
            core_out.at[t], core_in.at[t], core_send.at[t], core_recv.at[t],
            device_id=partner, device_id_type=MESH,
        )

    def core_start(t):
        core_out[t] = acc[1 - core, t].astype(BF)
        core_copy(t).start()

    def rows_of(index):
        return pl.ds(pl.multiple_of(index * PIECE, PIECE), PIECE)

    def core_sum(group):
        for t in range(3 * group, 3 * group + 3):
            core_copy(t).wait_recv()
            part[t * 256 : t * 256 + 256] = (acc[core, t] + core_in[t].astype(F32)).astype(BF)

    def scatter_start(group):
        core_sum(group)
        for h, w in around:
            pltpu.make_async_remote_copy(
                part.at[rows_of(group * 16 + h * 4 + w)], scatter.at[group * 16 + spot],
                big_send.at[0], big_recv.at[group],
                device_id=(tm, h, w), device_id_type=MESH,
            ).start()
        scatter[group * 16 + spot] = part[rows_of(group * 16 + spot)]

    def big_wait(buf, sem, count):
        most = buf.at[pl.ds(0, count)]
        pltpu.make_async_copy(most, most, sem).wait()

    def add_plane(group):
        big_wait(scatter, big_recv.at[group], 15)
        rows = scatter[16 * group : 16 * group + 16].astype(F32)
        plane_sum[group] = jnp.sum(rows, axis=0).astype(BF)
        for to in others:
            pltpu.make_async_remote_copy(
                plane_sum.at[group], column_part.at[group, height],
                big_send.at[1], column_recv.at[group], device_id=to, device_id_type=MESH,
            ).start()
        column_part[group, height] = plane_sum[group]

    def spread(group):
        big_wait(column_part.at[group], column_recv.at[group], 3)
        place_here = gathered.at[group * 16 + spot]
        place_here[...] = jnp.sum(column_part[group].astype(F32), axis=0).astype(BF)
        for h, w in around:
            pltpu.make_async_remote_copy(
                place_here, place_here, big_send.at[2], gather_recv.at[group],
                device_id=(tm, h, w), device_id_type=MESH,
            ).start()

    def swap_copy(group):
        span = pl.ds(group * 16, 16)
        return pltpu.make_async_remote_copy(
            gathered.at[span], gathered_2.at[span], last_send.at[group], last_recv.at[group],
            device_id=partner, device_id_type=MESH,
        )

    def keep_copies(group):
        span = pl.ds(group * 16, 16)
        return (
            pltpu.make_async_copy(gathered.at[span], half_out.at[span], store_sem.at[4 + group]),
            pltpu.make_async_copy(gathered_2.at[span], other_out.at[span], store_sem.at[8 + group]),
        )

    def taps(low, high):
        @pl.loop(low, high)
        def _(t):
            d = space_tap(t)
            acc[0, t] = d[:, :128]
            acc[1, t] = d[:, 128:]
            core_start(t)

    for t in range(9, 12):
        core_start(t)
    features_back(0)
    features_parts()

    scatter_start(3)
    taps(0, 4)
    scatter_start(0)
    add_plane(3)
    taps(4, 7)
    scatter_start(1)
    add_plane(0)
    taps(7, 9)
    for n in range(4):
        pl.when(tm < 7)(to_previous(n).wait_recv)
    features_back(1)
    scatter_start(2)
    spread(3)
    spread(0)
    add_plane(1)
    input_back(0)
    add_plane(2)
    spread(1)
    input_back(1, functools.partial(spread, 2))

    grad_scale = float(CELLS) ** -0.5
    chan_wait(1, chan_recv)
    param_out[...] = jnp.sum(chan_p[...], axis=0) * grad_scale

    for group in (3, 0, 1, 2):
        big_wait(gathered, gather_recv.at[group], 15)
        swap_copy(group).start()
        keep_copies(group)[0].start()
    for group in (3, 0, 1, 2):
        swap_copy(group).wait_recv()
        keep_copies(group)[1].start()

    for kind in range(2):
        for p in range(2):
            halo_sent(kind, p)
    for n in range(4):
        pl.when(tm < 7)(to_next(n).wait_send)
        pl.when(tm > 0)(to_previous(n).wait_send)
    for copy in frames_on:
        pl.when(tm < 7)(copy.wait_send)
    share_wait(0, stat_send)
    share_wait(1, stat_send)
    chan_wait(0, chan_send)
    chan_wait(1, chan_send)

    @pl.loop(0, 12)
    def _(t):
        core_copy(t).wait_send()

    big_wait(scatter, big_send.at[0], 60)
    big_wait(scatter, big_send.at[1], 12)
    big_wait(gathered, big_send.at[2], 60)
    for group in range(4):
        swap_copy(group).wait_send()
        for copy in keep_copies(group):
            copy.wait()
    for copy in stores:
        copy.wait()


def finish(
    grad_in, half, other, params, grad_input, space_out, time_out, gain_out, shift_out
):
    core = lax.rem(lax.axis_index("tm"), 2)
    step = pl.program_id(0)
    grad_scale = float(CELLS) ** -0.5
    grad_input[...] = grad_in[...]
    shift_out[...] = jnp.concatenate([params[0:1], params[1:2]], axis=1)
    gain_out[...] = jnp.concatenate([params[2:3], params[3:4]], axis=1)

    def put(out):
        a = half[...].reshape(3, C, 128).astype(F32) * grad_scale
        b = other[...].reshape(3, C, 128).astype(F32) * grad_scale
        out[:, :, :128] = jnp.where(core == 0, a, b)
        out[:, :, 128:] = jnp.where(core == 0, b, a)

    pl.when(step < 3)(functools.partial(put, space_out))
    pl.when(step == 3)(functools.partial(put, time_out))


def body(frames, history, cotangent, space_weight, time_weight, norm_gain, norm_shift):
    hbm = pl.BlockSpec(memory_space=pl.ANY)
    vmem = pl.BlockSpec(memory_space=pltpu.VMEM)
    dma = pltpu.SemaphoreType.DMA
    chunks = jax.ShapeDtypeStruct((CHIPS, PIECE, 128), BF)
    grad_input, half, other, params = pl.pallas_call(
        kernel,
        out_shape=(
            jax.ShapeDtypeStruct((4, 32, 32, C), BF),
            chunks,
            chunks,
            jax.ShapeDtypeStruct((4, 128), F32),
        ),
        in_specs=[hbm] * 5 + [vmem] * 2,
        out_specs=(hbm, hbm, hbm, vmem),
        scratch_shapes=[
            pltpu.VMEM((3, 2, 34, 64, C), BF),
            pltpu.VMEM((3, 34, 64, C), BF),
            pltpu.VMEM((3, 2, 34, 64, C), BF),
            pltpu.VMEM((2, 32, 64, C), BF),
            pltpu.VMEM((3, 32, 64, C), BF),
            pltpu.VMEM((2, 32, 64, C), F32),
            pltpu.VMEM((2, 32, 64, C), F32),
            pltpu.VMEM((3, 32, 64, C), BF),
            pltpu.VMEM((2, 32, 64, C), BF),
            pltpu.VMEM((2, 32, 64, C), BF),
            pltpu.VMEM((9 * C, C), BF),
            pltpu.VMEM((9 * C, C), BF),
            pltpu.VMEM((3 * C, C), BF),
            pltpu.VMEM((3 * C, C), BF),
            pltpu.VMEM((2, 2, 2, 64, C), BF),
            pltpu.VMEM((2, 2, 2, 96, C), BF),
            pltpu.VMEM((2, 96, C), BF),
            pltpu.VMEM((2, 12, C, 128), F32),
            pltpu.VMEM((8, C), F32),
            pltpu.VMEM((2, DEVICES, 1, 128), F32),
            pltpu.VMEM((8, 4, 128), F32),
            pltpu.VMEM((16, 4, 128), F32),
            pltpu.VMEM((12, C, 128), BF),
            pltpu.VMEM((12, C, 128), BF),
            pltpu.VMEM((12 * C, 128), BF),
            pltpu.VMEM((CHIPS, PIECE, 128), BF),
            pltpu.VMEM((4, PIECE, 128), BF),
            pltpu.VMEM((4, 4, PIECE, 128), BF),
            pltpu.VMEM((CHIPS, PIECE, 128), BF),
            pltpu.VMEM((CHIPS, PIECE, 128), BF),
            dma((12,)),
            dma((12,)),
            dma((2,)),
            dma((2,)),
            dma((2, 2, 8)),
            dma((2, 2, 8)),
            dma((4,)),
            dma((4,)),
            dma((4,)),
            dma((4,)),
            dma((2,)),
            dma((2,)),
            dma((2,)),
            dma((2,)),
            dma((12,)),
            dma((12,)),
            dma((3,)),
            dma((4,)),
            dma((4,)),
            dma((4,)),
            dma((4,)),
            dma((4,)),
            pltpu.SemaphoreType.REGULAR,
        ],
        compiler_params=pltpu.CompilerParams(
            collective_id=0, has_side_effects=True, vmem_limit_bytes=58 << 20
        ),
        name="decoder_block_backward",
    )(
        frames,
        history,
        cotangent,
        space_weight.reshape(9 * C, C),
        time_weight.reshape(3 * C, C),
        norm_gain.reshape(1, C),
        norm_shift.reshape(1, C),
    )
    grad_input, space_grad, time_grad, gain_grad, shift_grad = pl.pallas_call(
        finish,
        out_shape=(
            jax.ShapeDtypeStruct((4, 32, 32, C), BF),
            jax.ShapeDtypeStruct((9, C, C), F32),
            jax.ShapeDtypeStruct((3, C, C), F32),
            jax.ShapeDtypeStruct((1, C), F32),
            jax.ShapeDtypeStruct((1, C), F32),
        ),
        grid=(4,),
        in_specs=[
            pl.BlockSpec((1, 32, 32, C), lambda n: (n, 0, 0, 0)),
            pl.BlockSpec((16, PIECE, 128), lambda n: (n, 0, 0)),
            pl.BlockSpec((16, PIECE, 128), lambda n: (n, 0, 0)),
            pl.BlockSpec((4, 128), lambda n: (0, 0)),
        ],
        out_specs=(
            pl.BlockSpec((1, 32, 32, C), lambda n: (n, 0, 0, 0)),
            pl.BlockSpec((3, C, C), lambda n: (jnp.minimum(n, 2), 0, 0)),
            pl.BlockSpec((3, C, C), lambda n: (0, 0, 0)),
            pl.BlockSpec((1, C), lambda n: (0, 0)),
            pl.BlockSpec((1, C), lambda n: (0, 0)),
        ),
        compiler_params=pltpu.CompilerParams(vmem_limit_bytes=58 << 20),
        name="scale_and_store",
    )(grad_input, half, other, params)
    return (
        grad_input,
        space_grad.reshape(3, 3, C, C),
        time_grad,
        gain_grad.reshape(C),
        shift_grad.reshape(C),
    )


def solution(mesh):
    split = P("tm", "ha", "wa", None)
    in_specs = (split, P(None, "ha", "wa", None), split, P(), P(), P(), P())
    out_specs = (split, P(), P(), P(), P())
    return jax.shard_map(body, mesh=mesh, in_specs=in_specs, out_specs=out_specs, check_vma=False)
```
